32 devices in a mesh: groups: 2 (over y), seq: 8 (over z, x), head: 2 (over core).
Axes of the slice: x: 2, y: 2, z: 4, core: 2. Of those that a mesh axis runs over, the one named last changes fastest.
Arguments:
- queries: bfloat16 [12288, 4096], P(('groups', 'seq'), 'head'), parts along dimension 0, may hold values from -500 to 500
- text_rows: bfloat16 [128, 2048], P(('groups', 'seq')), parts along dimension 0, may hold values from -6 to 6
- null_rows: bfloat16 [16, 2048], replicated, may hold values from -6 to 6
- kv_weight: bfloat16 [2048, 2, 4096], P('seq', None, 'head'), may hold values from -0.125 to 0.125
- prompt_lengths: int32 [16], P('groups'), parts along dimension 0, may hold values from 1 to 16, 64 in all
- block_owner: int32 [16], P(('groups', 'seq')), parts along dimension 0, may hold values from 0 to 7
- uncond_flags: int32 [16], P(('groups', 'seq')), parts along dimension 0, may hold values 0 or 1
Outputs:
- context: bfloat16 [12288, 4096], P(('groups', 'seq'), 'head'), parts along dimension 0
The draws below stay inside these ranges and needn't reach their ends.
There are 2 independent parts, one for each index of `groups`. The reference program is written for one: setup_inputs(seed, part) draws one part's arguments, and reference() takes and returns one part's arrays. A program takes and returns all parts, laid end to end along the dimension named above; an argument that names none is the same for every part. Nothing has to cross between parts.
Inputs may be any that keep to these rules, and one draw needn't show every extreme that they name: `prompt_lengths`: prompt j holds the text rows after those of prompts 0 to j - 1; the lengths sum to 64.
All inputs are finite; a program needn't handle non-finite values. No bound on the sum of `uncond_flags` on one device may be relied on, other than what follows from the above.
Results may differ from the reference program's by a relative error of at most 0.012.
Values may be sent and summed in bfloat16 or wider, within the bound.
No kernel may reach another device: no remote copies, remote signals or barrier semaphores. Data moves between devices by JAX's collectives and lax.ppermute only.
A program may use at most 128 MiB of HBM per device.

```python
import math
import jax
import jax.numpy as jnp
import numpy as np
from jax import lax

DT = 2048
HEADS = 32
HDIM = 128
REQS = 8
NULL_LEN = 16
TOK_DEV = 768
D = 4096
TXT = 64
KEYS = 80
TOKENS = 6144
BLOCKS = 8


def draw_queries(key, part):
    key = jax.random.fold_in(key, 11)
    key_base = jax.random.fold_in(key, 0)
    full_shape = (TOKENS, D)
    normal_part = jnp.clip(jax.random.normal(key_base, full_shape, jnp.float32), -6.0, 6.0)
    return normal_part.astype(jnp.bfloat16)


def set_ends(array, own_key, low, largest):
    spot = [jax.random.randint(jax.random.fold_in(own_key, axis), (), 0, length) for axis, length in enumerate(array.shape)]
    widest = array.shape.index(max(array.shape))
    neighbour = spot[:widest] + [(spot[widest] + 1) % array.shape[widest]] + spot[widest + 1:]
    return array.at[tuple(spot)].set(low).at[tuple(neighbour)].set(largest)


def block_levels(stream_key, shape, pieces, least, high):
    factor_of = 1.0
    for dim, blocks in pieces:
        steps = jax.random.uniform(jax.random.fold_in(jax.random.fold_in(stream_key, 6), dim), (blocks,), jnp.float32, least / len(pieces), high / len(pieces))
        factor_of = factor_of * jnp.repeat(jnp.exp(steps), shape[dim] // blocks).reshape((-1,) + (1,) * (len(shape) - 1 - dim))
    return factor_of


def length_profile(number_of, total, limit, lean):
    portions = [(1 << 20) // math.isqrt(standing ** lean) + 1 for standing in range(2, number_of + 1)]
    spare, counts = total - limit - (number_of - 1), [1] * (number_of - 1)
    while spare > 0:
        movable = [i for i in range(number_of - 1) if counts[i] < limit]
        pool, remaining = sum([portions[i] for i in movable]), spare
        for i in movable:
            extra = min(limit - counts[i], max(1, remaining * portions[i] // pool), spare)
            counts[i] = counts[i] + extra
            spare = spare - extra
    return np.array([limit] + counts)


def uneven_parts(key, count, total, most, lean):
    if count == 2:
        one = jax.random.randint(key, (), max(1, total - most), min(most, total - 1) + 1)
        return jnp.stack([one, total - one])
    sizes = jnp.asarray(length_profile(count, total, most, lean), jnp.int32)
    couples = (count - 1) // 2
    source_of, taker = sizes[1:1 + 2 * couples:2], sizes[2:2 + 2 * couples:2]
    margin = jnp.minimum(source_of - 1, most - taker)
    shifted = jax.random.randint(jax.random.fold_in(key, 1), (couples,), 0, 1 << 20) % (margin + 1)
    sizes = sizes.at[1:1 + 2 * couples:2].set(source_of - shifted).at[2:2 + 2 * couples:2].set(taker + shifted)
    return sizes[jax.random.permutation(jax.random.fold_in(key, 2), count)]


def bell_draw(stream_key, dims, spread, limit, cuts=(), kind=jnp.bfloat16):
    entries = spread * jax.random.normal(stream_key, dims, jnp.float32)
    if cuts:
        entries = entries * block_levels(stream_key, dims, cuts, -0.22, 0.18)
    return jnp.clip(entries, -limit, limit).astype(kind)


def setup_inputs(seed: int = 0, part: int = 0) -> dict:
    splits = jax.random.split(jax.random.key(seed), 8)
    own_keys = jax.random.split(jax.random.fold_in(splits[7], part), 8)
    queries = draw_queries(jax.random.fold_in(jax.random.fold_in(splits[7], part), 71), part)
    text_rows = bell_draw(own_keys[1], (TXT, DT), 1.0, 6.0, ((0, 8),))
    null_rows = bell_draw(splits[2], (NULL_LEN, DT), 1.0, 6.0)
    kv_weight = bell_draw(splits[3], (DT, 2, D), DT ** -0.5, 0.125, ((0, 8), (2, 2)))
    prompt_lengths = uneven_parts(own_keys[4], REQS, TXT, TXT // 4, 2).astype(jnp.int32)
    block_owner = set_ends(jax.random.randint(own_keys[5], (BLOCKS,), 0, REQS), jax.random.fold_in(own_keys[5], 1), 0, REQS - 1).astype(jnp.int32)
    uncond_flags = set_ends((jax.random.randint(own_keys[6], (BLOCKS,), 0, 2) < 1).astype(jnp.int32), jax.random.fold_in(own_keys[6], 1), 0, 1)
    return {"queries": queries, "text_rows": text_rows, "null_rows": null_rows, "kv_weight": kv_weight, "prompt_lengths": prompt_lengths, "block_owner": block_owner, "uncond_flags": uncond_flags}


def reference(queries, text_rows, null_rows, kv_weight, prompt_lengths, block_owner, uncond_flags):
    flat_weight = kv_weight.reshape(DT, 2 * D)
    text_kv = jnp.dot(text_rows, flat_weight, preferred_element_type=jnp.float32).astype(jnp.bfloat16)
    null_kv = jnp.dot(null_rows, flat_weight, preferred_element_type=jnp.float32).astype(jnp.bfloat16)
    keys_values = jnp.concatenate([text_kv, null_kv], axis=0)
    key_heads = keys_values[:, :D].astype(jnp.float32).reshape(KEYS, HEADS, HDIM)
    value_heads = keys_values[:, D:].astype(jnp.float32).reshape(KEYS, HEADS, HDIM)
    prompt_ends = jnp.cumsum(prompt_lengths).astype(jnp.int32)
    text_index = jnp.arange(TXT, dtype=jnp.int32)
    segment = jnp.sum((text_index[:, None] >= prompt_ends[None, :]).astype(jnp.int32), axis=1).astype(jnp.int32)
    segment_all = jnp.concatenate([segment, jnp.full((NULL_LEN,), -1, jnp.int32)])
    is_null = jnp.arange(KEYS, dtype=jnp.int32) >= TXT
    score_scale = HDIM ** -0.5
    query_blocks = queries.reshape(BLOCKS, TOK_DEV, HEADS, HDIM)

    def attend(inputs):
        query_block, request, uncond = inputs
        allowed = jnp.where(uncond == 1, is_null, segment_all == request)
        scores = jnp.einsum("qhd,khd->hqk", query_block.astype(jnp.float32), key_heads) * score_scale
        scores = jnp.where(allowed[None, None, :], scores, jnp.float32(-1e30))
        row_max = jnp.max(scores, axis=-1, keepdims=True)
        weights_exp = jnp.exp(scores - row_max)
        row_total = jnp.sum(weights_exp, axis=-1, keepdims=True)
        probs = lax.optimization_barrier((weights_exp / row_total).astype(jnp.bfloat16)).astype(jnp.float32)
        context = jnp.einsum("hqk,khd->qhd", probs, value_heads)
        return context.reshape(TOK_DEV, D).astype(jnp.bfloat16)

    context = lax.map(attend, (query_blocks, block_owner, uncond_flags))
    return context.reshape(TOKENS, D)
```

```python
import functools

import jax
import jax.numpy as jnp
from jax import lax
from jax.experimental import pallas as pl
from jax.experimental.pallas import tpu as pltpu
from jax.sharding import PartitionSpec as P

HDIM = 128
NULL_LEN = 16
SCALE = HDIM ** (-0.5)
VMEM_LIMIT = 48 * 1024 * 1024
NEG = -1e30


def gather_plan(queries, text_rows, null_rows, kv_weight, prompt_lengths, block_owner, uncond_flags):
    features_dev = kv_weight.shape[0]
    half_width = kv_weight.shape[2]
    text_dev = text_rows.shape[0]
    flat_weight = kv_weight.reshape(features_dev, 2 * half_width)
    text_cols = lax.all_to_all(text_rows, "seq", split_axis=1, concat_axis=0, tiled=True)
    own_rows = lax.psum_scatter(
        jnp.dot(text_cols, flat_weight, preferred_element_type=jnp.float32),
        "seq",
        scatter_dimension=0,
        tiled=True,
    )
    null_cols = lax.dynamic_slice_in_dim(
        null_rows, lax.axis_index("seq") * features_dev, features_dev, 1
    )
    null_part = jnp.dot(null_cols, flat_weight, preferred_element_type=jnp.float32)
    null_sum = lax.psum(null_part, "seq")
    own_kv = own_rows.astype(jnp.bfloat16).reshape(text_dev, 2, half_width)
    null_kv = null_sum.astype(jnp.bfloat16).reshape(NULL_LEN, 2, half_width)
    all_text = lax.all_gather(own_kv, "seq", axis=0, tiled=True)
    text_total = all_text.shape[0]
    heads_dev = half_width // HDIM
    keys_local = jnp.concatenate([all_text[:, 0], null_kv[:, 0]], axis=0).reshape(
        -1, heads_dev, HDIM
    )
    values_local = jnp.concatenate([all_text[:, 1], null_kv[:, 1]], axis=0).reshape(
        -1, heads_dev, HDIM
    )
    prompt_ends = jnp.cumsum(prompt_lengths)
    text_index = jnp.arange(text_total, dtype=jnp.int32)
    segment = jnp.sum((text_index[:, None] >= prompt_ends[None, :]).astype(jnp.int32), axis=1)
    segment_all = jnp.concatenate([segment, jnp.full((NULL_LEN,), -1, jnp.int32)])
    is_null = jnp.arange(text_total + NULL_LEN, dtype=jnp.int32) >= text_total
    allowed = jnp.where(uncond_flags[0] == 1, is_null, segment_all == block_owner[0])
    row_count = queries.shape[0]
    query_heads = queries.reshape(row_count, heads_dev, HDIM)
    scores = (
        jnp.einsum("qhd,khd->hqk", query_heads, keys_local, preferred_element_type=jnp.float32)
        * SCALE
    )
    scores = jnp.where(allowed[None, None, :], scores, jnp.float32(NEG))
    row_max = jnp.max(scores, axis=-1, keepdims=True)
    weights_exp = jnp.exp(scores - row_max)
    row_total = jnp.sum(weights_exp, axis=-1, keepdims=True)
    probs = (weights_exp / row_total).astype(jnp.bfloat16)
    context = jnp.einsum("hqk,khd->qhd", probs, values_local, preferred_element_type=jnp.float32)
    return context.reshape(row_count, half_width).astype(jnp.bfloat16)


def swap(x, n, mask):
    return lax.ppermute(x, "seq", [(i, i ^ mask) for i in range(n)])


def project_kernel(order, pos_ref, len_ref, null_ref, w_ref, pack_ref, send_k, keep_k, send_v, keep_v):
    n = len(order)
    pos = pos_ref[0]
    text_dev = pack_ref.shape[1] // 2
    rows = n * NULL_LEN
    packs = [pack_ref[jnp.bitwise_xor(pos, m)] for m in order]
    pack = jnp.concatenate(packs, axis=0)
    code = jnp.concatenate(
        [p.astype(jnp.float32)[text_dev:, :128] for p in packs for _ in range(2)], axis=0
    ).astype(jnp.int32)
    reqs = len_ref.shape[0]
    uncond = code >= reqs
    owner = jnp.where(uncond, code - reqs, code)
    start = jnp.zeros_like(owner)
    running = jnp.int32(0)
    for r in range(reqs):
        start = jnp.where(owner == r, running, start)
        running = running + len_ref[r]
    wanted = start + lax.broadcasted_iota(jnp.int32, (rows, 128), 0) % NULL_LEN
    col = lax.broadcasted_iota(jnp.int32, (rows, 128), 1)
    held = jnp.full((rows, 128), -1, jnp.int32)
    for slot, m in enumerate(order):
        first = slot * 2 * text_dev
        base = jnp.bitwise_xor(pos, m) * text_dev - first
        held = jnp.where((col >= first) & (col < first + text_dev), col + base, held)
    pick = (held == wanted).astype(jnp.float32).astype(jnp.bfloat16)
    text_sel = jnp.dot(pick, pack, preferred_element_type=jnp.float32)
    null_sel = jnp.concatenate([null_ref[...].astype(jnp.float32)] * n, axis=0)
    wide = jnp.concatenate([uncond] * (null_sel.shape[1] // 128), axis=1)
    sel = jnp.where(wide, null_sel, text_sel).astype(jnp.bfloat16)
    half = rows // 2
    width = send_k.shape[1]
    for kind, (send, keep) in enumerate(((send_k, keep_k), (send_v, keep_v))):
        for c in range(0, width, 512):
            part = jnp.dot(
                sel,
                w_ref[:, kind * width + c : kind * width + c + 512],
                preferred_element_type=jnp.float32,
            )
            send[:, c : c + 512] = part[:half].astype(jnp.bfloat16)
            keep[:, c : c + 512] = part[half:]


def spread_heads(kept_ref, got_ref, wide_ref):
    total = kept_ref[...] + got_ref[...].astype(jnp.float32)
    keys, width = total.shape
    heads = width // HDIM
    total = total.astype(jnp.bfloat16).astype(jnp.float32)
    head = lax.broadcasted_iota(jnp.int32, (heads, width), 0)
    col = lax.broadcasted_iota(jnp.int32, (heads, width), 1)
    mine = (col // HDIM) == head
    for key in range(keys):
        block = jnp.where(mine, jnp.broadcast_to(total[key : key + 1], (heads, width)), 0.0)
        wide_ref[key * heads : (key + 1) * heads] = block.astype(jnp.bfloat16)


def probs_kernel(len_ref, own_ref, flag_ref, q_ref, kept_ref, got_ref, out_ref, wide_ref):
    heads = q_ref.shape[1] // HDIM
    spread_heads(kept_ref, got_ref, wide_ref)
    count = jnp.int32(0)
    for r in range(len_ref.shape[0]):
        count = jnp.where(own_ref[0] == r, len_ref[r], count)
    count = jnp.where(flag_ref[0] == 1, NULL_LEN, count)
    block = 256
    for first in range(0, q_ref.shape[0], block):
        scores = lax.dot_general(
            q_ref[first : first + block],
            wide_ref[...],
            (((1,), (1,)), ((), ())),
            preferred_element_type=jnp.float32,
        )
        scores = scores * SCALE
        key = lax.broadcasted_iota(jnp.int32, scores.shape, 1) // heads
        scores = jnp.where(key < count, scores, NEG)
        parts = [scores[:, c : c + 128] for c in range(0, scores.shape[1], 128)]
        top = functools.reduce(jnp.maximum, parts)
        step = heads
        while step < 128:
            top = jnp.maximum(top, pltpu.roll(top, step, 1))
            step *= 2
        parts = [jnp.exp(p - top) for p in parts]
        total = functools.reduce(jnp.add, parts)
        step = heads
        while step < 128:
            total = total + pltpu.roll(total, step, 1)
            step *= 2
        out_ref[first : first + block] = jnp.concatenate(
            [p / total for p in parts], axis=1
        ).astype(jnp.bfloat16)


def context_kernel(p_ref, kept_ref, got_ref, out_ref, wide_ref):
    @pl.when(pl.program_id(0) == 0)
    def _():
        spread_heads(kept_ref, got_ref, wide_ref)

    block = out_ref.shape[0]
    first = pl.multiple_of(pl.program_id(0) * block, block)
    out_ref[...] = jnp.dot(
        p_ref[pl.ds(first, block)], wide_ref[...], preferred_element_type=jnp.float32
    ).astype(jnp.bfloat16)


def select_plan(n, queries, text_rows, null_rows, kv_weight, prompt_lengths, block_owner, uncond_flags):
    features = kv_weight.shape[0]
    width = kv_weight.shape[2]
    rows = queries.shape[0]
    reqs = prompt_lengths.shape[0]
    heads = width // HDIM
    pos = lax.axis_index("seq").astype(jnp.int32)
    code = (block_owner[0] + reqs * uncond_flags[0]).astype(jnp.bfloat16)
    packed = jnp.concatenate([text_rows, jnp.full(text_rows.shape, code, jnp.bfloat16)], axis=0)
    packed = packed.reshape(-1, n, features).transpose(1, 0, 2)
    packs = lax.all_to_all(packed, "seq", split_axis=0, concat_axis=0, tiled=True)
    null_cols = lax.dynamic_slice_in_dim(null_rows, pos * features, features, 1)
    flat_weight = kv_weight.reshape(features, 2 * width)
    order = [7, 3, 5, 1, 6, 2, 4, 0]
    half = n * NULL_LEN // 2
    sent = jax.ShapeDtypeStruct((half, width), jnp.bfloat16)
    kept = jax.ShapeDtypeStruct((half, width), jnp.float32)
    smem = pl.BlockSpec(memory_space=pltpu.SMEM)
    vmem = pl.BlockSpec(memory_space=pltpu.VMEM)
    params = pltpu.CompilerParams(vmem_limit_bytes=VMEM_LIMIT)
    send_k, keep_k, send_v, keep_v = pl.pallas_call(
        functools.partial(project_kernel, order),
        out_shape=[sent, kept] * 2,
        in_specs=[smem, smem, vmem, vmem, vmem],
        out_specs=[vmem] * 4,
        compiler_params=params,
        cost_estimate=pl.CostEstimate(
            flops=2 * 2 * half * features * 2 * width,
            bytes_accessed=8 * features * width,
            transcendentals=0,
        ),
        name="project",
    )(pos.reshape(1), prompt_lengths, null_cols, flat_weight, packs)

    def reduce_parts(send, keep):
        for mask in (1, 2):
            total = keep + swap(send, n, mask).astype(jnp.float32)
            cut = total.shape[0] // 2
            send, keep = total[:cut].astype(jnp.bfloat16), total[cut:]
        return keep, swap(send, n, 4)

    k_parts = reduce_parts(send_k, keep_k)
    v_parts = reduce_parts(send_v, keep_v)

    lanes = heads * NULL_LEN
    probs = pl.pallas_call(
        probs_kernel,
        out_shape=jax.ShapeDtypeStruct((rows, lanes), jnp.bfloat16),
        in_specs=[smem] * 3 + [vmem] * 3,
        out_specs=vmem,
        scratch_shapes=[pltpu.VMEM((lanes, width), jnp.bfloat16)],
        compiler_params=params,
        cost_estimate=pl.CostEstimate(
            flops=2 * rows * width * lanes, bytes_accessed=2 * rows * width, transcendentals=rows * lanes
        ),
        name="probs",
    )(prompt_lengths, block_owner, uncond_flags, queries, *k_parts)
    block = 256
    return pl.pallas_call(
        context_kernel,
        out_shape=jax.ShapeDtypeStruct((rows, width), jnp.bfloat16),
        grid=(rows // block,),
        in_specs=[vmem] * 3,
        out_specs=pl.BlockSpec((block, width), lambda i: (i, 0)),
        scratch_shapes=[pltpu.VMEM((lanes, width), jnp.bfloat16)],
        compiler_params=params,
        cost_estimate=pl.CostEstimate(
            flops=2 * rows * width * lanes, bytes_accessed=2 * rows * width, transcendentals=0
        ),
        name="context",
    )(probs, *v_parts)


def solution(mesh):
    n = mesh.shape["seq"]

    def per_device(queries, text_rows, null_rows, kv_weight, *rest):
        longest = n * text_rows.shape[0] // 4
        few = n == 8 and longest == NULL_LEN and text_rows.shape[0] == 8
        if few:
            return select_plan(n, queries, text_rows, null_rows, kv_weight, *rest)
        return gather_plan(queries, text_rows, null_rows, kv_weight, *rest)

    placed = (
        P(("groups", "seq"), "head"),
        P(("groups", "seq"), None),
        P(),
        P("seq", None, "head"),
        P("groups"),
        P(("groups", "seq")),
        P(("groups", "seq")),
    )
    return jax.shard_map(
        per_device,
        mesh=mesh,
        in_specs=placed,
        out_specs=P(("groups", "seq"), "head"),
        check_vma=False,
    )
```

```python
import functools

import jax
import jax.numpy as jnp
from jax import lax
from jax.experimental import pallas as pl
from jax.experimental.pallas import tpu as pltpu
from jax.sharding import PartitionSpec as P

HDIM = 128
NULL_LEN = 16
SCALE = HDIM ** (-0.5)
VMEM_LIMIT = 48 * 1024 * 1024
NEG = -1e30


def gather_plan(queries, text_rows, null_rows, kv_weight, prompt_lengths, block_owner, uncond_flags):
    features_dev = kv_weight.shape[0]
    half_width = kv_weight.shape[2]
    text_dev = text_rows.shape[0]
    flat_weight = kv_weight.reshape(features_dev, 2 * half_width)
    text_cols = lax.all_to_all(text_rows, "seq", split_axis=1, concat_axis=0, tiled=True)
    own_rows = lax.psum_scatter(
        jnp.dot(text_cols, flat_weight, preferred_element_type=jnp.float32),
        "seq",
        scatter_dimension=0,
        tiled=True,
    )
    null_cols = lax.dynamic_slice_in_dim(
        null_rows, lax.axis_index("seq") * features_dev, features_dev, 1
    )
    null_part = jnp.dot(null_cols, flat_weight, preferred_element_type=jnp.float32)
    null_sum = lax.psum(null_part, "seq")
    own_kv = own_rows.astype(jnp.bfloat16).reshape(text_dev, 2, half_width)
    null_kv = null_sum.astype(jnp.bfloat16).reshape(NULL_LEN, 2, half_width)
    all_text = lax.all_gather(own_kv, "seq", axis=0, tiled=True)
    text_total = all_text.shape[0]
    heads_dev = half_width // HDIM
    keys_local = jnp.concatenate([all_text[:, 0], null_kv[:, 0]], axis=0).reshape(
        -1, heads_dev, HDIM
    )
    values_local = jnp.concatenate([all_text[:, 1], null_kv[:, 1]], axis=0).reshape(
        -1, heads_dev, HDIM
    )
    prompt_ends = jnp.cumsum(prompt_lengths)
    text_index = jnp.arange(text_total, dtype=jnp.int32)
    segment = jnp.sum((text_index[:, None] >= prompt_ends[None, :]).astype(jnp.int32), axis=1)
    segment_all = jnp.concatenate([segment, jnp.full((NULL_LEN,), -1, jnp.int32)])
    is_null = jnp.arange(text_total + NULL_LEN, dtype=jnp.int32) >= text_total
    allowed = jnp.where(uncond_flags[0] == 1, is_null, segment_all == block_owner[0])
    row_count = queries.shape[0]
    query_heads = queries.reshape(row_count, heads_dev, HDIM)
    scores = (
        jnp.einsum("qhd,khd->hqk", query_heads, keys_local, preferred_element_type=jnp.float32)
        * SCALE
    )
    scores = jnp.where(allowed[None, None, :], scores, jnp.float32(NEG))
    row_max = jnp.max(scores, axis=-1, keepdims=True)
    weights_exp = jnp.exp(scores - row_max)
    row_total = jnp.sum(weights_exp, axis=-1, keepdims=True)
    probs = (weights_exp / row_total).astype(jnp.bfloat16)
    context = jnp.einsum("hqk,khd->qhd", probs, values_local, preferred_element_type=jnp.float32)
    return context.reshape(row_count, half_width).astype(jnp.bfloat16)


def swap(x, n, mask):
    return lax.ppermute(x, "seq", [(i, i ^ mask) for i in range(n)])


SOURCES = (0, 4, 2, 6, 1, 5, 3, 7)
TARGETS = (7, 3, 5, 1, 6, 2, 4, 0)


def project_kernel(
    pos_ref, len_ref, null_ref, w_ref, text_ref, code_ref, got_ref, send_k, keep_k, send_v, keep_v
):
    features = text_ref.shape[1]
    text_dev = 2 * text_ref.shape[0] // len(SOURCES)
    rows = len(TARGETS) * NULL_LEN
    pos = pos_ref[0]
    got = got_ref[...].astype(jnp.float32)
    text = jnp.concatenate([text_ref[...].astype(jnp.float32), got[:, :features]], axis=0)
    codes = jnp.concatenate([code_ref[...].astype(jnp.float32), got[:, features:]], axis=0)
    repeat = NULL_LEN // text_dev
    code = jnp.concatenate(
        [
            codes[SOURCES.index(m) * text_dev : (SOURCES.index(m) + 1) * text_dev]
            for m in TARGETS
            for _ in range(repeat)
        ],
        axis=0,
    ).astype(jnp.int32)
    reqs = len_ref.shape[0]
    uncond = code >= reqs
    owner = jnp.where(uncond, code - reqs, code)
    start = jnp.zeros_like(owner)
    running = jnp.int32(0)
    for r in range(reqs):
        start = jnp.where(owner == r, running, start)
        running = running + len_ref[r]
    wanted = start + lax.broadcasted_iota(jnp.int32, (rows, 128), 0) % NULL_LEN
    col = lax.broadcasted_iota(jnp.int32, (rows, 128), 1)
    held = jnp.full((rows, 128), -1, jnp.int32)
    for slot, m in enumerate(SOURCES):
        first = slot * text_dev
        base = jnp.bitwise_xor(pos, m) * text_dev - first
        held = jnp.where((col >= first) & (col < first + text_dev), col + base, held)
    pick = (held == wanted).astype(jnp.float32).astype(jnp.bfloat16)
    spare = jnp.zeros((128 - text.shape[0], features), jnp.float32)
    text = jnp.concatenate([text, spare], axis=0).astype(jnp.bfloat16)
    text_sel = jnp.dot(pick, text, preferred_element_type=jnp.float32)
    null_sel = jnp.concatenate([null_ref[...].astype(jnp.float32)] * len(TARGETS), axis=0)
    wide = jnp.concatenate([uncond] * (features // 128), axis=1)
    sel = jnp.where(wide, null_sel, text_sel).astype(jnp.bfloat16)
    half = rows // 2
    quarter = rows // 4
    width = send_k.shape[1]
    for c in range(0, width, 512):
        cols = slice(c, c + 512)
        part = jnp.dot(sel, w_ref[:, cols], preferred_element_type=jnp.float32)
        send_k[:, cols] = part[:half].astype(jnp.bfloat16)
        keep_k[:, cols] = part[half:]
    for c in range(0, width, 512):
        cols = slice(c, c + 512)
        part = jnp.dot(
            sel, w_ref[:, width + c : width + c + 512], preferred_element_type=jnp.float32
        )
        send_v[:quarter, cols] = part[:quarter].astype(jnp.bfloat16)
        send_v[quarter:, cols] = part[half : half + quarter].astype(jnp.bfloat16)
        keep_v[:quarter, cols] = part[quarter:half]
        keep_v[quarter:, cols] = part[half + quarter :]


def spread_heads(kept_ref, got_ref, wide_ref):
    total = kept_ref[...] + got_ref[...].astype(jnp.float32)
    keys, width = total.shape
    heads = width // HDIM
    total = total.astype(jnp.bfloat16).astype(jnp.float32)
    head = lax.broadcasted_iota(jnp.int32, (heads, width), 0)
    col = lax.broadcasted_iota(jnp.int32, (heads, width), 1)
    mine = (col // HDIM) == head
    for key in range(keys):
        block = jnp.where(mine, jnp.broadcast_to(total[key : key + 1], (heads, width)), 0.0)
        wide_ref[key * heads : (key + 1) * heads] = block.astype(jnp.bfloat16)


def probs_kernel(len_ref, own_ref, flag_ref, q_ref, kept_ref, got_ref, out_ref, wide_ref):
    heads = q_ref.shape[1] // HDIM
    spread_heads(kept_ref, got_ref, wide_ref)
    count = jnp.int32(0)
    for r in range(len_ref.shape[0]):
        count = jnp.where(own_ref[0] == r, len_ref[r], count)
    count = jnp.where(flag_ref[0] == 1, NULL_LEN, count)
    block = 256
    for first in range(0, q_ref.shape[0], block):
        scores = lax.dot_general(
            q_ref[first : first + block],
            wide_ref[...],
            (((1,), (1,)), ((), ())),
            preferred_element_type=jnp.float32,
        )
        scores = scores * SCALE
        key = lax.broadcasted_iota(jnp.int32, scores.shape, 1) // heads
        scores = jnp.where(key < count, scores, NEG)
        parts = [scores[:, c : c + 128] for c in range(0, scores.shape[1], 128)]
        top = functools.reduce(jnp.maximum, parts)
        step = heads
        while step < 128:
            top = jnp.maximum(top, pltpu.roll(top, step, 1))
            step *= 2
        parts = [jnp.exp(p - top) for p in parts]
        total = functools.reduce(jnp.add, parts)
        step = heads
        while step < 128:
            total = total + pltpu.roll(total, step, 1)
            step *= 2
        out_ref[first : first + block] = jnp.concatenate(
            [p / total for p in parts], axis=1
        ).astype(jnp.bfloat16)


def context_kernel(p_ref, kept_ref, got_ref, out_ref, wide_ref):
    @pl.when(pl.program_id(0) == 0)
    def _():
        spread_heads(kept_ref, got_ref, wide_ref)

    block = out_ref.shape[0]
    first = pl.multiple_of(pl.program_id(0) * block, block)
    out_ref[...] = jnp.dot(
        p_ref[pl.ds(first, block)], wide_ref[...], preferred_element_type=jnp.float32
    ).astype(jnp.bfloat16)


def select_plan(n, queries, text_rows, null_rows, kv_weight, prompt_lengths, block_owner, uncond_flags):
    features = kv_weight.shape[0]
    width = kv_weight.shape[2]
    rows = queries.shape[0]
    reqs = prompt_lengths.shape[0]
    heads = width // HDIM
    pos = lax.axis_index("seq").astype(jnp.int32)
    text = text_rows
    code = (block_owner[0] + reqs * uncond_flags[0]).astype(jnp.bfloat16)
    code = jnp.full((text_rows.shape[0], 128), code, jnp.bfloat16)
    for mask in (4, 2, 1):
        cut = text.shape[1] // 2
        side = (pos // mask) % 2
        theirs = lax.dynamic_slice_in_dim(text, (1 - side) * cut, cut, 1)
        text = lax.dynamic_slice_in_dim(text, side * cut, cut, 1)
        got = swap(jnp.concatenate([theirs, code], axis=1), n, mask)
        if mask > 1:
            text = jnp.concatenate([text, got[:, :cut]], axis=0)
            code = jnp.concatenate([code, got[:, cut:]], axis=0)
    null_cols = lax.dynamic_slice_in_dim(null_rows, pos * features, features, 1)
    flat_weight = kv_weight.reshape(features, 2 * width)
    half = n * NULL_LEN // 2
    sent = jax.ShapeDtypeStruct((half, width), jnp.bfloat16)
    kept = jax.ShapeDtypeStruct((half, width), jnp.float32)
    smem = pl.BlockSpec(memory_space=pltpu.SMEM)
    vmem = pl.BlockSpec(memory_space=pltpu.VMEM)
    params = pltpu.CompilerParams(vmem_limit_bytes=VMEM_LIMIT)
    send_k, keep_k, send_v, keep_v = pl.pallas_call(
        project_kernel,
        out_shape=[sent, kept] * 2,
        in_specs=[smem, smem] + [vmem] * 5,
        out_specs=[vmem] * 4,
        compiler_params=params,
        cost_estimate=pl.CostEstimate(
            flops=2 * 2 * half * features * 2 * width,
            bytes_accessed=8 * features * width,
            transcendentals=0,
        ),
        name="project",
    )(pos.reshape(1), prompt_lengths, null_cols, flat_weight, text, code, got)

    def reduce_parts(send, keep, masks):
        for mask in masks:
            total = keep + swap(send, n, mask).astype(jnp.float32)
            cut = total.shape[0] // 2
            send, keep = total[:cut].astype(jnp.bfloat16), total[cut:]
        return keep, swap(send, n, 4)

    k_parts = reduce_parts(send_k, keep_k, (1, 2))
    v_parts = reduce_parts(send_v, keep_v, (2, 1))

    lanes = heads * NULL_LEN
    probs = pl.pallas_call(
        probs_kernel,
        out_shape=jax.ShapeDtypeStruct((rows, lanes), jnp.bfloat16),
        in_specs=[smem] * 3 + [vmem] * 3,
        out_specs=vmem,
        scratch_shapes=[pltpu.VMEM((lanes, width), jnp.bfloat16)],
        compiler_params=params,
        cost_estimate=pl.CostEstimate(
            flops=2 * rows * width * lanes, bytes_accessed=2 * rows * width, transcendentals=rows * lanes
        ),
        name="probs",
    )(prompt_lengths, block_owner, uncond_flags, queries, *k_parts)
    block = 256
    return pl.pallas_call(
        context_kernel,
        out_shape=jax.ShapeDtypeStruct((rows, width), jnp.bfloat16),
        grid=(rows // block,),
        in_specs=[vmem] * 3,
        out_specs=pl.BlockSpec((block, width), lambda i: (i, 0)),
        scratch_shapes=[pltpu.VMEM((lanes, width), jnp.bfloat16)],
        compiler_params=params,
        cost_estimate=pl.CostEstimate(
            flops=2 * rows * width * lanes, bytes_accessed=2 * rows * width, transcendentals=0
        ),
        name="context",
    )(probs, *v_parts)


def solution(mesh):
    n = mesh.shape["seq"]

    def per_device(queries, text_rows, null_rows, kv_weight, *rest):
        longest = n * text_rows.shape[0] // 4
        few = n == 8 and longest == NULL_LEN and text_rows.shape[0] == 8
        if few:
            return select_plan(n, queries, text_rows, null_rows, kv_weight, *rest)
        return gather_plan(queries, text_rows, null_rows, kv_weight, *rest)

    placed = (
        P(("groups", "seq"), "head"),
        P(("groups", "seq"), None),
        P(),
        P("seq", None, "head"),
        P("groups"),
        P(("groups", "seq")),
        P(("groups", "seq")),
    )
    return jax.shard_map(
        per_device,
        mesh=mesh,
        in_specs=placed,
        out_specs=P(("groups", "seq"), "head"),
        check_vma=False,
    )
```

```python
import functools

import jax
import jax.numpy as jnp
from jax import lax
from jax.experimental import pallas as pl
from jax.experimental.pallas import tpu as pltpu
from jax.sharding import PartitionSpec as P

HDIM = 128
NULL_LEN = 16
SCALE = HDIM ** (-0.5)
VMEM_LIMIT = 48 * 1024 * 1024
NEG = -1e30


def gather_plan(queries, text_rows, null_rows, kv_weight, prompt_lengths, block_owner, uncond_flags):
    features_dev = kv_weight.shape[0]
    half_width = kv_weight.shape[2]
    text_dev = text_rows.shape[0]
    flat_weight = kv_weight.reshape(features_dev, 2 * half_width)
    text_cols = lax.all_to_all(text_rows, "seq", split_axis=1, concat_axis=0, tiled=True)
    own_rows = lax.psum_scatter(
        jnp.dot(text_cols, flat_weight, preferred_element_type=jnp.float32),
        "seq",
        scatter_dimension=0,
        tiled=True,
    )
    null_cols = lax.dynamic_slice_in_dim(
        null_rows, lax.axis_index("seq") * features_dev, features_dev, 1
    )
    null_part = jnp.dot(null_cols, flat_weight, preferred_element_type=jnp.float32)
    null_sum = lax.psum(null_part, "seq")
    own_kv = own_rows.astype(jnp.bfloat16).reshape(text_dev, 2, half_width)
    null_kv = null_sum.astype(jnp.bfloat16).reshape(NULL_LEN, 2, half_width)
    all_text = lax.all_gather(own_kv, "seq", axis=0, tiled=True)
    text_total = all_text.shape[0]
    heads_dev = half_width // HDIM
    keys_local = jnp.concatenate([all_text[:, 0], null_kv[:, 0]], axis=0).reshape(
        -1, heads_dev, HDIM
    )
    values_local = jnp.concatenate([all_text[:, 1], null_kv[:, 1]], axis=0).reshape(
        -1, heads_dev, HDIM
    )
    prompt_ends = jnp.cumsum(prompt_lengths)
    text_index = jnp.arange(text_total, dtype=jnp.int32)
    segment = jnp.sum((text_index[:, None] >= prompt_ends[None, :]).astype(jnp.int32), axis=1)
    segment_all = jnp.concatenate([segment, jnp.full((NULL_LEN,), -1, jnp.int32)])
    is_null = jnp.arange(text_total + NULL_LEN, dtype=jnp.int32) >= text_total
    allowed = jnp.where(uncond_flags[0] == 1, is_null, segment_all == block_owner[0])
    row_count = queries.shape[0]
    query_heads = queries.reshape(row_count, heads_dev, HDIM)
    scores = (
        jnp.einsum("qhd,khd->hqk", query_heads, keys_local, preferred_element_type=jnp.float32)
        * SCALE
    )
    scores = jnp.where(allowed[None, None, :], scores, jnp.float32(NEG))
    row_max = jnp.max(scores, axis=-1, keepdims=True)
    weights_exp = jnp.exp(scores - row_max)
    row_total = jnp.sum(weights_exp, axis=-1, keepdims=True)
    probs = (weights_exp / row_total).astype(jnp.bfloat16)
    context = jnp.einsum("hqk,khd->qhd", probs, values_local, preferred_element_type=jnp.float32)
    return context.reshape(row_count, half_width).astype(jnp.bfloat16)


def swap(x, n, mask):
    return lax.ppermute(x, "seq", [(i, i ^ mask) for i in range(n)])


SOURCES = (0, 4, 2, 6, 1, 5, 3, 7)
TARGETS = (7, 3, 5, 1, 6, 2, 4, 0)


def weight_kernel(w_ref, after_ref, out_ref):
    del after_ref
    rows, width = out_ref.shape
    flat = w_ref.reshape(rows, width)
    for c in range(0, width, 512):
        out_ref[:, c : c + 512] = flat[:, c : c + 512]


def project_kernel(
    pos_ref, len_ref, null_ref, w0_ref, w1_ref, held_ref, send_k, keep_k, send_v, keep_v, count_ref
):
    features = null_ref.shape[1]
    text_dev = held_ref.shape[0] // len(SOURCES)
    rows = len(TARGETS) * NULL_LEN
    pos = pos_ref[0]
    text = held_ref[:, :features]
    codes = held_ref[:, features:].astype(jnp.float32)
    code = jnp.concatenate(
        [
            codes[SOURCES.index(m) * text_dev : (SOURCES.index(m) + 1) * text_dev]
            for m in TARGETS
            for _ in range(NULL_LEN // text_dev)
        ],
        axis=0,
    ).astype(jnp.int32)
    reqs = len_ref.shape[0]
    uncond = code >= reqs
    owner = jnp.where(uncond, code - reqs, code)
    start = jnp.zeros_like(owner)
    running = jnp.int32(0)
    for r in range(reqs):
        start = jnp.where(owner == r, running, start)
        running = running + len_ref[r]
    wanted = start + lax.broadcasted_iota(jnp.int32, (rows, 128), 0) % NULL_LEN
    col = lax.broadcasted_iota(jnp.int32, (rows, 128), 1)
    held = jnp.full((rows, 128), -1, jnp.int32)
    for slot, m in enumerate(SOURCES):
        first = slot * text_dev
        base = jnp.bitwise_xor(pos, m) * text_dev - first
        held = jnp.where((col >= first) & (col < first + text_dev), col + base, held)
    pick = (held == wanted).astype(jnp.float32).astype(jnp.bfloat16)
    text = jnp.concatenate([text, jnp.zeros((128 - text.shape[0], features), jnp.bfloat16)], axis=0)
    text_sel = jnp.dot(pick, text, preferred_element_type=jnp.float32)
    null_sel = jnp.concatenate([null_ref[...].astype(jnp.float32)] * len(TARGETS), axis=0)
    wide = jnp.concatenate([uncond] * (features // 128), axis=1)
    sel = jnp.where(wide, null_sel, text_sel).astype(jnp.bfloat16)
    own = TARGETS.index(0) * NULL_LEN
    count = jnp.zeros_like(owner[own : own + 8])
    for r in range(reqs):
        count = jnp.where(owner[own : own + 8] == r, len_ref[r], count)
    count_ref[...] = jnp.where(uncond[own : own + 8], NULL_LEN, count)
    feature = lax.broadcasted_iota(jnp.int32, (features, 2 * features), 0)
    place = lax.broadcasted_iota(jnp.int32, (features, 2 * features), 1)
    spread = [
        jnp.dot(
            sel,
            (place == 2 * feature + kind).astype(jnp.float32).astype(jnp.bfloat16),
            preferred_element_type=jnp.float32,
        )
        for kind in range(2)
    ]
    spread = jnp.concatenate(spread, axis=0).astype(jnp.bfloat16)
    half = rows // 2
    quarter = rows // 4
    width = send_k.shape[1]
    for c in range(0, width, 512):
        cols = slice(c, c + 512)
        w_ref, at = (w0_ref, c) if c < w0_ref.shape[1] else (w1_ref, c - w0_ref.shape[1])
        part = jnp.dot(spread, w_ref[:, at : at + 512], preferred_element_type=jnp.float32)
        send_k[:, cols] = part[:half].astype(jnp.bfloat16)
        keep_k[:, cols] = part[half:rows]
        send_v[:quarter, cols] = part[rows : rows + quarter].astype(jnp.bfloat16)
        send_v[quarter:, cols] = part[rows + half : rows + half + quarter].astype(jnp.bfloat16)
        keep_v[:quarter, cols] = part[rows + quarter : rows + half]
        keep_v[quarter:, cols] = part[rows + half + quarter :]


def spread_heads(kept_ref, got_ref, wide_ref):
    total = kept_ref[...] + got_ref[...].astype(jnp.float32)
    keys, width = total.shape
    heads = width // HDIM
    total = total.astype(jnp.bfloat16).astype(jnp.float32)
    head = lax.broadcasted_iota(jnp.int32, (heads, width), 0)
    col = lax.broadcasted_iota(jnp.int32, (heads, width), 1)
    mine = (col // HDIM) == head
    for key in range(keys):
        block = jnp.where(mine, jnp.broadcast_to(total[key : key + 1], (heads, width)), 0.0)
        wide_ref[key * heads : (key + 1) * heads] = block.astype(jnp.bfloat16)


def probs_kernel(count_ref, q_ref, kept_ref, got_ref, out_ref, wide_ref):
    heads = q_ref.shape[1] // HDIM
    spread_heads(kept_ref, got_ref, wide_ref)
    count = jnp.broadcast_to(jnp.concatenate([count_ref[:1]] * (out_ref.shape[1] // 128), axis=1), (256, out_ref.shape[1]))
    block = 256
    for first in range(0, q_ref.shape[0], block):
        scores = lax.dot_general(
            q_ref[first : first + block],
            wide_ref[...],
            (((1,), (1,)), ((), ())),
            preferred_element_type=jnp.float32,
        )
        scores = scores * SCALE
        key = lax.broadcasted_iota(jnp.int32, scores.shape, 1) // heads
        scores = jnp.where(key < count, scores, NEG)
        parts = [scores[:, c : c + 128] for c in range(0, scores.shape[1], 128)]
        top = functools.reduce(jnp.maximum, parts)
        step = heads
        while step < 128:
            top = jnp.maximum(top, pltpu.roll(top, step, 1))
            step *= 2
        parts = [jnp.exp(p - top) for p in parts]
        total = functools.reduce(jnp.add, parts)
        step = heads
        while step < 128:
            total = total + pltpu.roll(total, step, 1)
            step *= 2
        out_ref[first : first + block] = jnp.concatenate(
            [p / total for p in parts], axis=1
        ).astype(jnp.bfloat16)


def context_kernel(p_ref, kept_ref, got_ref, out_hbm, wide_ref, out_ref, sems):
    spread_heads(kept_ref, got_ref, wide_ref)
    block = out_ref.shape[0] // sems.shape[0]
    copies = []
    for i in range(sems.shape[0]):
        rows = pl.ds(i * block, block)
        out_ref[rows] = jnp.dot(
            p_ref[rows], wide_ref[...], preferred_element_type=jnp.float32
        ).astype(jnp.bfloat16)
        copies.append(pltpu.make_async_copy(out_ref.at[rows], out_hbm.at[rows], sems.at[i]))
        copies[-1].start()
    for copy in copies:
        copy.wait()


def select_plan(n, queries, text_rows, null_rows, kv_weight, prompt_lengths, block_owner, uncond_flags):
    features = kv_weight.shape[0]
    width = kv_weight.shape[2]
    rows = queries.shape[0]
    reqs = prompt_lengths.shape[0]
    heads = width // HDIM
    pos = lax.axis_index("seq").astype(jnp.int32)
    smem = pl.BlockSpec(memory_space=pltpu.SMEM)
    vmem = pl.BlockSpec(memory_space=pltpu.VMEM)
    anywhere = pl.BlockSpec(memory_space=pl.ANY)
    params = pltpu.CompilerParams(vmem_limit_bytes=VMEM_LIMIT)

    def lay_out(first, after):
        return pl.pallas_call(
            weight_kernel,
            out_shape=jax.ShapeDtypeStruct((2 * features, width // 2), jnp.bfloat16),
            grid=(1,),
            in_specs=[
                pl.BlockSpec((features, 2, width // 2), lambda i: (0, 0, first)),
                anywhere,
            ],
            out_specs=pl.BlockSpec((2 * features, width // 2), lambda i: (0, 0)),
            compiler_params=params,
            cost_estimate=pl.CostEstimate(
                flops=0, bytes_accessed=4 * features * width, transcendentals=0
            ),
            name="weight",
        )(kv_weight, after)

    def swap_last(x, mask):
        pairs = [(2 * i + 1, 2 * (i ^ mask) + 1) for i in range(n)]
        return lax.ppermute(x, ("seq", "head"), pairs)

    text = text_rows
    code = (block_owner[0] + reqs * uncond_flags[0]).astype(jnp.bfloat16)
    code = jnp.full((text_rows.shape[0], 128), code, jnp.bfloat16)
    weights = []
    for stage, mask in enumerate((4, 2, 1)):
        cut = text.shape[1] // 2
        side = (pos // mask) % 2
        theirs = lax.dynamic_slice_in_dim(text, (1 - side) * cut, cut, 1)
        text = lax.dynamic_slice_in_dim(text, side * cut, cut, 1)
        send = jnp.concatenate([theirs, code], axis=1)
        if stage:
            send, weights[-1] = lax.optimization_barrier((send, weights[-1]))
        got = swap_last(send, mask)
        if stage < 2:
            weights.append(lay_out(stage, send))
        text = jnp.concatenate([text, got[:, :cut]], axis=0)
        code = jnp.concatenate([code, got[:, cut:]], axis=0)
    held = jnp.concatenate([text, code], axis=1)
    handed = lax.ppermute(held, ("seq", "head"), [(2 * i + 1, 2 * i) for i in range(n)])
    held = jnp.where(lax.axis_index("head") == 1, held, handed)
    null_cols = lax.dynamic_slice_in_dim(null_rows, pos * features, features, 1)
    half = n * NULL_LEN // 2
    sent = jax.ShapeDtypeStruct((half, width), jnp.bfloat16)
    kept = jax.ShapeDtypeStruct((half, width), jnp.float32)
    send_k, keep_k, send_v, keep_v, count = pl.pallas_call(
        project_kernel,
        out_shape=[sent, kept] * 2 + [jax.ShapeDtypeStruct((8, 128), jnp.int32)],
        in_specs=[smem, smem] + [vmem] * 4,
        out_specs=[vmem] * 5,
        compiler_params=params,
        cost_estimate=pl.CostEstimate(
            flops=2 * 2 * half * features * 2 * width,
            bytes_accessed=8 * features * width,
            transcendentals=0,
        ),
        name="project",
    )(pos.reshape(1), prompt_lengths, null_cols, *weights, held)

    def reduce_parts(send, keep, masks):
        for mask in masks:
            total = keep + swap(send, n, mask).astype(jnp.float32)
            cut = total.shape[0] // 2
            send, keep = total[:cut].astype(jnp.bfloat16), total[cut:]
        return keep, swap(send, n, 4)

    k_parts = reduce_parts(send_k, keep_k, (1, 2))
    v_parts = reduce_parts(send_v, keep_v, (2, 1))

    lanes = heads * NULL_LEN
    probs = pl.pallas_call(
        probs_kernel,
        out_shape=jax.ShapeDtypeStruct((rows, lanes), jnp.bfloat16),
        in_specs=[vmem] * 4,
        out_specs=vmem,
        scratch_shapes=[pltpu.VMEM((lanes, width), jnp.bfloat16)],
        compiler_params=params,
        cost_estimate=pl.CostEstimate(
            flops=2 * rows * width * lanes, bytes_accessed=2 * rows * width, transcendentals=rows * lanes
        ),
        name="probs",
    )(count, queries, *k_parts)
    return pl.pallas_call(
        context_kernel,
        out_shape=jax.ShapeDtypeStruct((rows, width), jnp.bfloat16),
        in_specs=[vmem] * 3,
        out_specs=anywhere,
        scratch_shapes=[
            pltpu.VMEM((lanes, width), jnp.bfloat16),
            pltpu.VMEM((rows, width), jnp.bfloat16),
            pltpu.SemaphoreType.DMA((6,)),
        ],
        compiler_params=params,
        cost_estimate=pl.CostEstimate(
            flops=2 * rows * width * lanes, bytes_accessed=2 * rows * width, transcendentals=0
        ),
        name="context",
    )(probs, *v_parts)


def solution(mesh):
    n = mesh.shape["seq"]

    def per_device(queries, text_rows, null_rows, kv_weight, *rest):
        longest = n * text_rows.shape[0] // 4
        few = n == 8 and mesh.shape["head"] == 2 and longest == NULL_LEN and text_rows.shape[0] == 8
        if few:
            return select_plan(n, queries, text_rows, null_rows, kv_weight, *rest)
        return gather_plan(queries, text_rows, null_rows, kv_weight, *rest)

    placed = (
        P(("groups", "seq"), "head"),
        P(("groups", "seq"), None),
        P(),
        P("seq", None, "head"),
        P("groups"),
        P(("groups", "seq")),
        P(("groups", "seq")),
    )
    return jax.shard_map(
        per_device,
        mesh=mesh,
        in_specs=placed,
        out_specs=P(("groups", "seq"), "head"),
        check_vma=False,
    )
```

```python
import functools

import jax
import jax.numpy as jnp
from jax import lax
from jax.experimental import pallas as pl
from jax.experimental.pallas import tpu as pltpu
from jax.sharding import PartitionSpec as P

HDIM = 128
NULL_LEN = 16
SCALE = HDIM ** (-0.5)
VMEM_LIMIT = 16 * 1024 * 1024
NEG = -1e30


def gather_plan(queries, text_rows, null_rows, kv_weight, prompt_lengths, block_owner, uncond_flags):
    features_dev = kv_weight.shape[0]
    half_width = kv_weight.shape[2]
    text_dev = text_rows.shape[0]
    flat_weight = kv_weight.reshape(features_dev, 2 * half_width)
    text_cols = lax.all_to_all(text_rows, "seq", split_axis=1, concat_axis=0, tiled=True)
    own_rows = lax.psum_scatter(
        jnp.dot(text_cols, flat_weight, preferred_element_type=jnp.float32),
        "seq",
        scatter_dimension=0,
        tiled=True,
    )
    null_cols = lax.dynamic_slice_in_dim(
        null_rows, lax.axis_index("seq") * features_dev, features_dev, 1
    )
    null_part = jnp.dot(null_cols, flat_weight, preferred_element_type=jnp.float32)
    null_sum = lax.psum(null_part, "seq")
    own_kv = own_rows.astype(jnp.bfloat16).reshape(text_dev, 2, half_width)
    null_kv = null_sum.astype(jnp.bfloat16).reshape(NULL_LEN, 2, half_width)
    all_text = lax.all_gather(own_kv, "seq", axis=0, tiled=True)
    text_total = all_text.shape[0]
    heads_dev = half_width // HDIM
    keys_local = jnp.concatenate([all_text[:, 0], null_kv[:, 0]], axis=0).reshape(
        -1, heads_dev, HDIM
    )
    values_local = jnp.concatenate([all_text[:, 1], null_kv[:, 1]], axis=0).reshape(
        -1, heads_dev, HDIM
    )
    prompt_ends = jnp.cumsum(prompt_lengths)
    text_index = jnp.arange(text_total, dtype=jnp.int32)
    segment = jnp.sum((text_index[:, None] >= prompt_ends[None, :]).astype(jnp.int32), axis=1)
    segment_all = jnp.concatenate([segment, jnp.full((NULL_LEN,), -1, jnp.int32)])
    is_null = jnp.arange(text_total + NULL_LEN, dtype=jnp.int32) >= text_total
    allowed = jnp.where(uncond_flags[0] == 1, is_null, segment_all == block_owner[0])
    row_count = queries.shape[0]
    query_heads = queries.reshape(row_count, heads_dev, HDIM)
    scores = (
        jnp.einsum("qhd,khd->hqk", query_heads, keys_local, preferred_element_type=jnp.float32)
        * SCALE
    )
    scores = jnp.where(allowed[None, None, :], scores, jnp.float32(NEG))
    row_max = jnp.max(scores, axis=-1, keepdims=True)
    weights_exp = jnp.exp(scores - row_max)
    row_total = jnp.sum(weights_exp, axis=-1, keepdims=True)
    probs = (weights_exp / row_total).astype(jnp.bfloat16)
    context = jnp.einsum("hqk,khd->qhd", probs, values_local, preferred_element_type=jnp.float32)
    return context.reshape(row_count, half_width).astype(jnp.bfloat16)


def swap(x, n, mask):
    return lax.ppermute(x, "seq", [(i, i ^ mask) for i in range(n)])


def keys_kernel(pos_ref, len_ref, null_ref, w_ref, rows_ref, send_ref, keep_ref, sel_ref, count_ref):
    features = null_ref.shape[1]
    rows = sel_ref.shape[0]
    total = rows_ref.shape[0]
    text_dev = total * NULL_LEN // rows
    reqs = len_ref.shape[0]
    held = rows_ref[...]
    held = jnp.concatenate([held, jnp.zeros((rows - total, held.shape[1]), held.dtype)], axis=0)
    row = lax.broadcasted_iota(jnp.int32, (rows, rows), 0)
    col = lax.broadcasted_iota(jnp.int32, (rows, rows), 1)
    slot = row // NULL_LEN
    flip = 7 - ((slot % 2) * 4 + (slot // 2 % 2) * 2 + slot // 4)
    first = jnp.bitwise_xor(flip, pos_ref[0]) * text_dev

    def take(which, columns):
        which = which.astype(jnp.float32).astype(jnp.bfloat16)
        return jnp.dot(which, columns, preferred_element_type=jnp.float32)

    code = take(col == first, held[:, features:]).astype(jnp.int32)
    uncond = code >= reqs
    owner = jnp.where(uncond, code - reqs, code)
    start = jnp.zeros_like(owner)
    length = jnp.zeros_like(owner)
    running = jnp.int32(0)
    for r in range(reqs):
        start = jnp.where(owner == r, running, start)
        length = jnp.where(owner == r, len_ref[r], length)
        running = running + len_ref[r]
    own = rows - NULL_LEN
    count_ref[...] = jnp.where(uncond, NULL_LEN, length)[own : own + 8]
    text_sel = take(col == start + row % NULL_LEN, held[:, :features])
    null_sel = jnp.concatenate([null_ref[...].astype(jnp.float32)] * (rows // NULL_LEN), axis=0)
    wide = jnp.concatenate([uncond] * (features // rows), axis=1)
    sel = jnp.where(wide, null_sel, text_sel).astype(jnp.bfloat16)
    sel_ref[...] = sel
    half = rows // 2
    width = send_ref.shape[1]
    for c in range(0, width, 512):
        cols = slice(c, c + 512)
        part = jnp.dot(sel, w_ref[:, cols], preferred_element_type=jnp.float32)
        send_ref[:, cols] = part[:half].astype(jnp.bfloat16)
        keep_ref[:, cols] = part[half:]


def values_kernel(sel_ref, w_ref, send_ref, keep_ref):
    quarter = sel_ref.shape[0] // 4
    width = send_ref.shape[1]
    for c in range(0, width, 512):
        cols = slice(c, c + 512)
        part = jnp.dot(
            sel_ref[...], w_ref[:, width + c : width + c + 512], preferred_element_type=jnp.float32
        )
        send_ref[:quarter, cols] = part[:quarter].astype(jnp.bfloat16)
        send_ref[quarter:, cols] = part[2 * quarter : 3 * quarter].astype(jnp.bfloat16)
        keep_ref[:quarter, cols] = part[quarter : 2 * quarter]
        keep_ref[quarter:, cols] = part[3 * quarter :]


def spread_heads(kept_ref, got_ref, cols):
    heads = kept_ref.shape[1] // HDIM
    total = kept_ref[:, cols] + got_ref[:, cols].astype(jnp.float32)
    keys, width = total.shape
    total = total.astype(jnp.bfloat16).astype(jnp.float32)
    head = lax.broadcasted_iota(jnp.int32, (heads, width), 0)
    col = lax.broadcasted_iota(jnp.int32, (heads, width), 1) + cols.start
    mine = (col // HDIM) == head
    blocks = [
        jnp.where(mine, jnp.broadcast_to(total[key : key + 1], (heads, width)), 0.0).astype(
            jnp.bfloat16
        )
        for key in range(keys)
    ]
    return jnp.concatenate(blocks, axis=0)


def probs_kernel(count_ref, q_ref, kept_ref, got_ref, out_ref, wide_ref):
    heads = q_ref.shape[1] // HDIM
    width = q_ref.shape[1]
    for c in range(0, width, 512):
        cols = slice(c, c + 512)
        wide_ref[:, cols] = spread_heads(kept_ref, got_ref, cols)
    count = jnp.broadcast_to(jnp.concatenate([count_ref[:1]] * (out_ref.shape[1] // 128), axis=1), (256, out_ref.shape[1]))
    block = 256
    for first in range(0, q_ref.shape[0], block):
        scores = lax.dot_general(
            q_ref[first : first + block],
            wide_ref[...],
            (((1,), (1,)), ((), ())),
            preferred_element_type=jnp.float32,
        )
        scores = scores * SCALE
        key = lax.broadcasted_iota(jnp.int32, scores.shape, 1) // heads
        scores = jnp.where(key < count, scores, NEG)
        parts = [scores[:, c : c + 128] for c in range(0, scores.shape[1], 128)]
        top = functools.reduce(jnp.maximum, parts)
        step = heads
        while step < 128:
            top = jnp.maximum(top, pltpu.roll(top, step, 1))
            step *= 2
        parts = [jnp.exp(p - top) for p in parts]
        total = functools.reduce(jnp.add, parts)
        step = heads
        while step < 128:
            total = total + pltpu.roll(total, step, 1)
            step *= 2
        out_ref[first : first + block] = jnp.concatenate(
            [p / total for p in parts], axis=1
        ).astype(jnp.bfloat16)


def context_kernel(p_ref, kept_ref, got_ref, out_hbm, out_ref, sems):
    chunk = out_ref.shape[1] // sems.shape[0]
    copies = []
    for i in range(sems.shape[0]):
        cols = slice(i * chunk, (i + 1) * chunk)
        out_ref[:, cols] = jnp.dot(
            p_ref[...], spread_heads(kept_ref, got_ref, cols), preferred_element_type=jnp.float32
        ).astype(jnp.bfloat16)
        copies.append(pltpu.make_async_copy(out_ref.at[:, cols], out_hbm.at[:, cols], sems.at[i]))
        copies[-1].start()
    for copy in copies:
        copy.wait()


def select_plan(n, queries, text_rows, null_rows, kv_weight, prompt_lengths, block_owner, uncond_flags):
    features = kv_weight.shape[0]
    width = kv_weight.shape[2]
    rows = queries.shape[0]
    reqs = prompt_lengths.shape[0]
    heads = width // HDIM
    pos = lax.axis_index("seq").astype(jnp.int32)
    smem = pl.BlockSpec(memory_space=pltpu.SMEM)
    vmem = pl.BlockSpec(memory_space=pltpu.VMEM)
    anywhere = pl.BlockSpec(memory_space=pl.ANY)
    params = pltpu.CompilerParams(vmem_limit_bytes=VMEM_LIMIT)
    text_dev = text_rows.shape[0]
    code = (block_owner[0] + reqs * uncond_flags[0]).astype(jnp.bfloat16)
    text = text_rows.reshape(text_dev, n, features).transpose(1, 0, 2)
    packed = jnp.concatenate([text, jnp.full((n, text_dev, 128), code, jnp.bfloat16)], axis=2)
    held = lax.all_to_all(packed, "seq", split_axis=0, concat_axis=0, tiled=True)
    held = held.reshape(n * text_dev, features + 128)
    null_cols = lax.dynamic_slice_in_dim(null_rows, pos * features, features, 1)
    weight = kv_weight.reshape(features, 2 * width)
    half = n * NULL_LEN // 2
    sent = jax.ShapeDtypeStruct((half, width), jnp.bfloat16)
    kept = jax.ShapeDtypeStruct((half, width), jnp.float32)
    estimate = pl.CostEstimate(
        flops=2 * 2 * half * features * width,
        bytes_accessed=2 * features * width,
        transcendentals=0,
    )
    send_k, keep_k, sel, count = pl.pallas_call(
        keys_kernel,
        out_shape=[
            sent,
            kept,
            jax.ShapeDtypeStruct((2 * half, features), jnp.bfloat16),
            jax.ShapeDtypeStruct((8, 128), jnp.int32),
        ],
        in_specs=[smem, smem] + [vmem] * 3,
        out_specs=[vmem] * 4,
        compiler_params=params,
        cost_estimate=estimate,
        name="keys",
    )(pos.reshape(1), prompt_lengths, null_cols, weight, held)
    send_v, keep_v = pl.pallas_call(
        values_kernel,
        out_shape=[sent, kept],
        in_specs=[vmem] * 2,
        out_specs=[vmem] * 2,
        compiler_params=params,
        cost_estimate=estimate,
        name="values",
    )(sel, weight)

    def reduce_parts(send, keep, masks):
        for mask in masks:
            total = keep + swap(send, n, mask).astype(jnp.float32)
            cut = total.shape[0] // 2
            send, keep = total[:cut].astype(jnp.bfloat16), total[cut:]
        return keep, swap(send, n, 4)

    k_parts = reduce_parts(send_k, keep_k, (1, 2))
    v_parts = reduce_parts(send_v, keep_v, (2, 1))

    lanes = heads * NULL_LEN
    probs = pl.pallas_call(
        probs_kernel,
        out_shape=jax.ShapeDtypeStruct((rows, lanes), jnp.bfloat16),
        in_specs=[vmem] * 4,
        out_specs=vmem,
        scratch_shapes=[pltpu.VMEM((lanes, width), jnp.bfloat16)],
        compiler_params=params,
        cost_estimate=pl.CostEstimate(
            flops=2 * rows * width * lanes, bytes_accessed=2 * rows * width, transcendentals=rows * lanes
        ),
        name="probs",
    )(count, queries, *k_parts)
    return pl.pallas_call(
        context_kernel,
        out_shape=jax.ShapeDtypeStruct((rows, width), jnp.bfloat16),
        in_specs=[vmem] * 3,
        out_specs=anywhere,
        scratch_shapes=[
            pltpu.VMEM((rows, width), jnp.bfloat16),
            pltpu.SemaphoreType.DMA((4,)),
        ],
        compiler_params=params,
        cost_estimate=pl.CostEstimate(
            flops=2 * rows * width * lanes, bytes_accessed=2 * rows * width, transcendentals=0
        ),
        name="context",
    )(probs, *v_parts)


def solution(mesh):
    n = mesh.shape["seq"]

    def per_device(queries, text_rows, null_rows, kv_weight, *rest):
        longest = n * text_rows.shape[0] // 4
        few = n == 8 and longest == NULL_LEN and text_rows.shape[0] == 8
        if few:
            return select_plan(n, queries, text_rows, null_rows, kv_weight, *rest)
        return gather_plan(queries, text_rows, null_rows, kv_weight, *rest)

    placed = (
        P(("groups", "seq"), "head"),
        P(("groups", "seq"), None),
        P(),
        P("seq", None, "head"),
        P("groups"),
        P(("groups", "seq")),
        P(("groups", "seq")),
    )
    return jax.shard_map(
        per_device,
        mesh=mesh,
        in_specs=placed,
        out_specs=P(("groups", "seq"), "head"),
        check_vma=False,
    )
```

```python
import functools

import jax
import jax.numpy as jnp
from jax import lax
from jax.experimental import pallas as pl
from jax.experimental.pallas import tpu as pltpu
from jax.sharding import PartitionSpec as P

HDIM = 128
NULL_LEN = 16
SCALE = HDIM ** (-0.5)
VMEM_LIMIT = 16 * 1024 * 1024
NEG = -1e30


def gather_plan(queries, text_rows, null_rows, kv_weight, prompt_lengths, block_owner, uncond_flags):
    features_dev = kv_weight.shape[0]
    half_width = kv_weight.shape[2]
    text_dev = text_rows.shape[0]
    flat_weight = kv_weight.reshape(features_dev, 2 * half_width)
    text_cols = lax.all_to_all(text_rows, "seq", split_axis=1, concat_axis=0, tiled=True)
    own_rows = lax.psum_scatter(
        jnp.dot(text_cols, flat_weight, preferred_element_type=jnp.float32),
        "seq",
        scatter_dimension=0,
        tiled=True,
    )
    null_cols = lax.dynamic_slice_in_dim(
        null_rows, lax.axis_index("seq") * features_dev, features_dev, 1
    )
    null_part = jnp.dot(null_cols, flat_weight, preferred_element_type=jnp.float32)
    null_sum = lax.psum(null_part, "seq")
    own_kv = own_rows.astype(jnp.bfloat16).reshape(text_dev, 2, half_width)
    null_kv = null_sum.astype(jnp.bfloat16).reshape(NULL_LEN, 2, half_width)
    all_text = lax.all_gather(own_kv, "seq", axis=0, tiled=True)
    text_total = all_text.shape[0]
    heads_dev = half_width // HDIM
    keys_local = jnp.concatenate([all_text[:, 0], null_kv[:, 0]], axis=0).reshape(
        -1, heads_dev, HDIM
    )
    values_local = jnp.concatenate([all_text[:, 1], null_kv[:, 1]], axis=0).reshape(
        -1, heads_dev, HDIM
    )
    prompt_ends = jnp.cumsum(prompt_lengths)
    text_index = jnp.arange(text_total, dtype=jnp.int32)
    segment = jnp.sum((text_index[:, None] >= prompt_ends[None, :]).astype(jnp.int32), axis=1)
    segment_all = jnp.concatenate([segment, jnp.full((NULL_LEN,), -1, jnp.int32)])
    is_null = jnp.arange(text_total + NULL_LEN, dtype=jnp.int32) >= text_total
    allowed = jnp.where(uncond_flags[0] == 1, is_null, segment_all == block_owner[0])
    row_count = queries.shape[0]
    query_heads = queries.reshape(row_count, heads_dev, HDIM)
    scores = (
        jnp.einsum("qhd,khd->hqk", query_heads, keys_local, preferred_element_type=jnp.float32)
        * SCALE
    )
    scores = jnp.where(allowed[None, None, :], scores, jnp.float32(NEG))
    row_max = jnp.max(scores, axis=-1, keepdims=True)
    weights_exp = jnp.exp(scores - row_max)
    row_total = jnp.sum(weights_exp, axis=-1, keepdims=True)
    probs = (weights_exp / row_total).astype(jnp.bfloat16)
    context = jnp.einsum("hqk,khd->qhd", probs, values_local, preferred_element_type=jnp.float32)
    return context.reshape(row_count, half_width).astype(jnp.bfloat16)


def swap(x, n, masks):
    pairs = [(2 * i + head, 2 * (i ^ masks[head]) + head) for i in range(n) for head in range(2)]
    return lax.ppermute(x, ("seq", "head"), pairs)


TARGETS = ((7, 3, 5, 1, 6, 2, 4, 0), (7, 3, 6, 2, 5, 1, 4, 0))


def keys_kernel(
    pos_ref, head_ref, len_ref, null_ref, w_ref, code_ref, rows_ref, send_ref, keep_ref, sel_ref, count_ref
):
    features = null_ref.shape[1]
    rows = sel_ref.shape[0]
    total = rows_ref.shape[0]
    text_dev = code_ref.shape[1]
    text = rows_ref[:, :features]
    text = jnp.concatenate([text, jnp.zeros((rows - total, features), text.dtype)], axis=0)
    codes = []
    for m, m_last in zip(*TARGETS):
        peer = jnp.bitwise_xor(pos_ref[0], jnp.where(head_ref[0] == 0, m, m_last))
        code = code_ref[peer][:, features:].astype(jnp.float32)
        codes += [code] * (NULL_LEN // text_dev)
    code = jnp.concatenate(codes, axis=0)
    reqs = len_ref.shape[1]
    uncond = code >= reqs
    owner = jnp.where(uncond, code - reqs, code)[:, :reqs]
    request = lax.broadcasted_iota(jnp.int32, owner.shape, 1).astype(jnp.float32)
    lengths = jnp.broadcast_to(len_ref[...].astype(jnp.float32), owner.shape)
    start = jnp.sum(jnp.where(request < owner, lengths, 0.0), axis=1, keepdims=True)
    length = jnp.sum(jnp.where(request == owner, lengths, 0.0), axis=1, keepdims=True)
    length = jnp.where(uncond, NULL_LEN, jnp.broadcast_to(length, uncond.shape))
    own = rows - NULL_LEN
    count_ref[...] = length[own : own + 8].astype(jnp.int32)
    row = lax.broadcasted_iota(jnp.int32, code.shape, 0) % NULL_LEN
    col = lax.broadcasted_iota(jnp.int32, code.shape, 1)
    pick = col.astype(jnp.float32) == start + row.astype(jnp.float32)
    pick = pick.astype(jnp.float32).astype(jnp.bfloat16)
    text_sel = jnp.dot(pick, text, preferred_element_type=jnp.float32)
    null_sel = jnp.concatenate([null_ref[...].astype(jnp.float32)] * (rows // NULL_LEN), axis=0)
    wide = jnp.concatenate([uncond] * (features // 128), axis=1)
    sel = jnp.where(wide, null_sel, text_sel).astype(jnp.bfloat16)
    sel_ref[...] = sel
    half = rows // 2
    width = send_ref.shape[1]
    for c in range(0, width, 512):
        cols = slice(c, c + 512)
        part = jnp.dot(sel, w_ref[:, cols], preferred_element_type=jnp.float32)
        send_ref[:, cols] = part[:half].astype(jnp.bfloat16)
        keep_ref[:, cols] = part[half:]


def values_kernel(sel_ref, w_ref, send_ref, keep_ref):
    quarter = sel_ref.shape[0] // 4
    width = send_ref.shape[1]
    for c in range(0, width, 512):
        cols = slice(c, c + 512)
        part = jnp.dot(
            sel_ref[...], w_ref[:, width + c : width + c + 512], preferred_element_type=jnp.float32
        )
        send_ref[:quarter, cols] = part[:quarter].astype(jnp.bfloat16)
        send_ref[quarter:, cols] = part[2 * quarter : 3 * quarter].astype(jnp.bfloat16)
        keep_ref[:quarter, cols] = part[quarter : 2 * quarter]
        keep_ref[quarter:, cols] = part[3 * quarter :]


def spread_heads(kept_ref, got_ref, cols):
    heads = kept_ref.shape[1] // HDIM
    total = kept_ref[:, cols] + got_ref[:, cols].astype(jnp.float32)
    keys, width = total.shape
    total = total.astype(jnp.bfloat16).astype(jnp.float32)
    head = lax.broadcasted_iota(jnp.int32, (heads, width), 0)
    col = lax.broadcasted_iota(jnp.int32, (heads, width), 1) + cols.start
    mine = (col // HDIM) == head
    blocks = [
        jnp.where(mine, jnp.broadcast_to(total[key : key + 1], (heads, width)), 0.0).astype(
            jnp.bfloat16
        )
        for key in range(keys)
    ]
    return jnp.concatenate(blocks, axis=0)


def probs_kernel(count_ref, q_ref, kept_ref, got_ref, out_ref, wide_ref):
    heads = q_ref.shape[1] // HDIM
    width = q_ref.shape[1]
    for c in range(0, width, 512):
        cols = slice(c, c + 512)
        wide_ref[:, cols] = spread_heads(kept_ref, got_ref, cols)
    count = jnp.broadcast_to(jnp.concatenate([count_ref[:1]] * (out_ref.shape[1] // 128), axis=1), (256, out_ref.shape[1]))
    block = 256
    for first in range(0, q_ref.shape[0], block):
        scores = lax.dot_general(
            q_ref[first : first + block],
            wide_ref[...],
            (((1,), (1,)), ((), ())),
            preferred_element_type=jnp.float32,
        )
        scores = scores * SCALE
        key = lax.broadcasted_iota(jnp.int32, scores.shape, 1) // heads
        scores = jnp.where(key < count, scores, NEG)
        parts = [scores[:, c : c + 128] for c in range(0, scores.shape[1], 128)]
        top = functools.reduce(jnp.maximum, parts)
        step = heads
        while step < 128:
            top = jnp.maximum(top, pltpu.roll(top, step, 1))
            step *= 2
        parts = [jnp.exp(p - top) for p in parts]
        total = functools.reduce(jnp.add, parts)
        step = heads
        while step < 128:
            total = total + pltpu.roll(total, step, 1)
            step *= 2
        out_ref[first : first + block] = jnp.concatenate(
            [p / total for p in parts], axis=1
        ).astype(jnp.bfloat16)


def context_kernel(p_ref, kept_ref, got_ref, out_hbm, out_ref, sems):
    chunk = out_ref.shape[1] // sems.shape[0]
    copies = []
    for i in range(sems.shape[0]):
        cols = slice(i * chunk, (i + 1) * chunk)
        out_ref[:, cols] = jnp.dot(
            p_ref[...], spread_heads(kept_ref, got_ref, cols), preferred_element_type=jnp.float32
        ).astype(jnp.bfloat16)
        copies.append(pltpu.make_async_copy(out_ref.at[:, cols], out_hbm.at[:, cols], sems.at[i]))
        copies[-1].start()
    for copy in copies:
        copy.wait()


def select_plan(n, queries, text_rows, null_rows, kv_weight, prompt_lengths, block_owner, uncond_flags):
    features = kv_weight.shape[0]
    width = kv_weight.shape[2]
    rows = queries.shape[0]
    reqs = prompt_lengths.shape[0]
    heads = width // HDIM
    pos = lax.axis_index("seq").astype(jnp.int32)
    smem = pl.BlockSpec(memory_space=pltpu.SMEM)
    vmem = pl.BlockSpec(memory_space=pltpu.VMEM)
    anywhere = pl.BlockSpec(memory_space=pl.ANY)
    params = pltpu.CompilerParams(vmem_limit_bytes=VMEM_LIMIT)
    text_dev = text_rows.shape[0]
    code = (block_owner[0] + reqs * uncond_flags[0]).astype(jnp.bfloat16)
    text = text_rows.reshape(text_dev, n, features).transpose(1, 0, 2)
    packed = jnp.concatenate([text, jnp.full((n, text_dev, 128), code, jnp.bfloat16)], axis=2)
    held = lax.all_to_all(packed, "seq", split_axis=0, concat_axis=0, tiled=True)
    null_cols = lax.dynamic_slice_in_dim(null_rows, pos * features, features, 1)
    weight = kv_weight.reshape(features, 2 * width)
    half = n * NULL_LEN // 2
    sent = jax.ShapeDtypeStruct((half, width), jnp.bfloat16)
    kept = jax.ShapeDtypeStruct((half, width), jnp.float32)
    estimate = pl.CostEstimate(
        flops=2 * 2 * half * features * width,
        bytes_accessed=2 * features * width,
        transcendentals=0,
    )
    send_k, keep_k, sel, count = pl.pallas_call(
        keys_kernel,
        out_shape=[
            sent,
            kept,
            jax.ShapeDtypeStruct((2 * half, features), jnp.bfloat16),
            jax.ShapeDtypeStruct((8, 128), jnp.int32),
        ],
        in_specs=[smem] * 2 + [vmem] * 5,
        out_specs=[vmem] * 4,
        compiler_params=params,
        cost_estimate=estimate,
        name="keys",
    )(
        pos.reshape(1),
        lax.axis_index("head").astype(jnp.int32).reshape(1),
        prompt_lengths.reshape(1, reqs),
        null_cols,
        weight,
        held,
        held.reshape(n * text_dev, features + 128),
    )
    send_v, keep_v = pl.pallas_call(
        values_kernel,
        out_shape=[sent, kept],
        in_specs=[vmem] * 2,
        out_specs=[vmem] * 2,
        compiler_params=params,
        cost_estimate=estimate,
        name="values",
    )(sel, weight)

    def reduce_parts(send, keep, masks):
        for mask in masks:
            total = keep + swap(send, n, mask).astype(jnp.float32)
            cut = total.shape[0] // 2
            send, keep = total[:cut].astype(jnp.bfloat16), total[cut:]
        return keep, swap(send, n, (4, 4))

    k_parts = reduce_parts(send_k, keep_k, ((1, 2), (2, 1)))
    v_parts = reduce_parts(send_v, keep_v, ((2, 1), (1, 2)))

    lanes = heads * NULL_LEN
    probs = pl.pallas_call(
        probs_kernel,
        out_shape=jax.ShapeDtypeStruct((rows, lanes), jnp.bfloat16),
        in_specs=[vmem] * 4,
        out_specs=vmem,
        scratch_shapes=[pltpu.VMEM((lanes, width), jnp.bfloat16)],
        compiler_params=params,
        cost_estimate=pl.CostEstimate(
            flops=2 * rows * width * lanes, bytes_accessed=2 * rows * width, transcendentals=rows * lanes
        ),
        name="probs",
    )(count, queries, *k_parts)
    return pl.pallas_call(
        context_kernel,
        out_shape=jax.ShapeDtypeStruct((rows, width), jnp.bfloat16),
        in_specs=[vmem] * 3,
        out_specs=anywhere,
        scratch_shapes=[
            pltpu.VMEM((rows, width), jnp.bfloat16),
            pltpu.SemaphoreType.DMA((4,)),
        ],
        compiler_params=params,
        cost_estimate=pl.CostEstimate(
            flops=2 * rows * width * lanes, bytes_accessed=2 * rows * width, transcendentals=0
        ),
        name="context",
    )(probs, *v_parts)


def solution(mesh):
    n = mesh.shape["seq"]

    def per_device(queries, text_rows, null_rows, kv_weight, *rest):
        longest = n * text_rows.shape[0] // 4
        few = n == 8 and mesh.shape["head"] == 2 and longest == NULL_LEN and text_rows.shape[0] == 8
        if few:
            return select_plan(n, queries, text_rows, null_rows, kv_weight, *rest)
        return gather_plan(queries, text_rows, null_rows, kv_weight, *rest)

    placed = (
        P(("groups", "seq"), "head"),
        P(("groups", "seq"), None),
        P(),
        P("seq", None, "head"),
        P("groups"),
        P(("groups", "seq")),
        P(("groups", "seq")),
    )
    return jax.shard_map(
        per_device,
        mesh=mesh,
        in_specs=placed,
        out_specs=P(("groups", "seq"), "head"),
        check_vma=False,
    )
```

```python
import functools

import jax
import jax.numpy as jnp
from jax import lax
from jax.experimental import pallas as pl
from jax.experimental.pallas import tpu as pltpu
from jax.sharding import PartitionSpec as P

HDIM = 128
NULL_LEN = 16
SCALE = HDIM ** (-0.5)
VMEM_LIMIT = 16 * 1024 * 1024
NEG = -1e30


def gather_plan(queries, text_rows, null_rows, kv_weight, prompt_lengths, block_owner, uncond_flags):
    features_dev = kv_weight.shape[0]
    half_width = kv_weight.shape[2]
    text_dev = text_rows.shape[0]
    flat_weight = kv_weight.reshape(features_dev, 2 * half_width)
    text_cols = lax.all_to_all(text_rows, "seq", split_axis=1, concat_axis=0, tiled=True)
    own_rows = lax.psum_scatter(
        jnp.dot(text_cols, flat_weight, preferred_element_type=jnp.float32),
        "seq",
        scatter_dimension=0,
        tiled=True,
    )
    null_cols = lax.dynamic_slice_in_dim(
        null_rows, lax.axis_index("seq") * features_dev, features_dev, 1
    )
    null_part = jnp.dot(null_cols, flat_weight, preferred_element_type=jnp.float32)
    null_sum = lax.psum(null_part, "seq")
    own_kv = own_rows.astype(jnp.bfloat16).reshape(text_dev, 2, half_width)
    null_kv = null_sum.astype(jnp.bfloat16).reshape(NULL_LEN, 2, half_width)
    all_text = lax.all_gather(own_kv, "seq", axis=0, tiled=True)
    text_total = all_text.shape[0]
    heads_dev = half_width // HDIM
    keys_local = jnp.concatenate([all_text[:, 0], null_kv[:, 0]], axis=0).reshape(
        -1, heads_dev, HDIM
    )
    values_local = jnp.concatenate([all_text[:, 1], null_kv[:, 1]], axis=0).reshape(
        -1, heads_dev, HDIM
    )
    prompt_ends = jnp.cumsum(prompt_lengths)
    text_index = jnp.arange(text_total, dtype=jnp.int32)
    segment = jnp.sum((text_index[:, None] >= prompt_ends[None, :]).astype(jnp.int32), axis=1)
    segment_all = jnp.concatenate([segment, jnp.full((NULL_LEN,), -1, jnp.int32)])
    is_null = jnp.arange(text_total + NULL_LEN, dtype=jnp.int32) >= text_total
    allowed = jnp.where(uncond_flags[0] == 1, is_null, segment_all == block_owner[0])
    row_count = queries.shape[0]
    query_heads = queries.reshape(row_count, heads_dev, HDIM)
    scores = (
        jnp.einsum("qhd,khd->hqk", query_heads, keys_local, preferred_element_type=jnp.float32)
        * SCALE
    )
    scores = jnp.where(allowed[None, None, :], scores, jnp.float32(NEG))
    row_max = jnp.max(scores, axis=-1, keepdims=True)
    weights_exp = jnp.exp(scores - row_max)
    row_total = jnp.sum(weights_exp, axis=-1, keepdims=True)
    probs = (weights_exp / row_total).astype(jnp.bfloat16)
    context = jnp.einsum("hqk,khd->qhd", probs, values_local, preferred_element_type=jnp.float32)
    return context.reshape(row_count, half_width).astype(jnp.bfloat16)


def swap(x, n, mask):
    return lax.ppermute(x, "seq", [(i, i ^ mask) for i in range(n)])


TARGETS = (7, 3, 6, 2, 5, 1, 4, 0)
MIDDLE = 5


def pack_kernel(reqs, owner_ref, flag_ref, text_hbm, out_hbm, code_ref, sems):
    places, _, width = out_hbm.shape
    features = width - 128
    copies = []
    for place in range(places):
        cols = pl.ds((place ^ MIDDLE) * features, features)
        copies.append(
            pltpu.make_async_copy(
                text_hbm.at[:, cols], out_hbm.at[place, :, pl.ds(0, features)], sems.at[place]
            )
        )
        copies[-1].start()
    code = (owner_ref[0] + reqs * flag_ref[0]).astype(jnp.float32)
    code_ref[...] = jnp.full(code_ref.shape, code, jnp.float32).astype(jnp.bfloat16)
    copies.append(
        pltpu.make_async_copy(code_ref, out_hbm.at[:, :, pl.ds(features, 128)], sems.at[places])
    )
    copies[-1].start()
    for copy in copies:
        copy.wait()


def keys_kernel(
    pos_ref, len_ref, null_ref, w_ref, code_ref, rows_ref, send_ref, keep_ref, sel_ref, count_ref
):
    features = null_ref.shape[1]
    rows = sel_ref.shape[0]
    total = rows_ref.shape[0]
    text_dev = code_ref.shape[1]
    text = rows_ref[:, :features]
    text = jnp.concatenate([text, jnp.zeros((rows - total, features), text.dtype)], axis=0)
    codes = []
    for m in TARGETS:
        code = code_ref[jnp.bitwise_xor(pos_ref[0], m ^ MIDDLE)][:, features:].astype(jnp.float32)
        codes += [code] * (NULL_LEN // text_dev)
    code = jnp.concatenate(codes, axis=0)
    reqs = len_ref.shape[1]
    uncond = code >= reqs
    owner = jnp.where(uncond, code - reqs, code)[:, :reqs]
    request = lax.broadcasted_iota(jnp.int32, owner.shape, 1).astype(jnp.float32)
    lengths = jnp.broadcast_to(len_ref[...].astype(jnp.float32), owner.shape)
    start = jnp.sum(jnp.where(request < owner, lengths, 0.0), axis=1, keepdims=True)
    length = jnp.sum(jnp.where(request == owner, lengths, 0.0), axis=1, keepdims=True)
    length = jnp.where(uncond, NULL_LEN, jnp.broadcast_to(length, uncond.shape))
    own = rows - NULL_LEN
    count_ref[...] = length[own : own + 8].astype(jnp.int32)
    row = lax.broadcasted_iota(jnp.int32, code.shape, 0) % NULL_LEN
    col = jnp.bitwise_xor(lax.broadcasted_iota(jnp.int32, code.shape, 1), MIDDLE * text_dev)
    pick = col.astype(jnp.float32) == start + row.astype(jnp.float32)
    pick = pick.astype(jnp.float32).astype(jnp.bfloat16)
    text_sel = jnp.dot(pick, text, preferred_element_type=jnp.float32)
    null_sel = jnp.concatenate([null_ref[...].astype(jnp.float32)] * (rows // NULL_LEN), axis=0)
    wide = jnp.concatenate([uncond] * (features // 128), axis=1)
    sel = jnp.where(wide, null_sel, text_sel).astype(jnp.bfloat16)
    sel_ref[...] = sel
    half = rows // 2
    width = send_ref.shape[1]
    for c in range(0, width, 512):
        cols = slice(c, c + 512)
        part = jnp.dot(sel, w_ref[:, cols], preferred_element_type=jnp.float32)
        send_ref[:, cols] = part[:half].astype(jnp.bfloat16)
        keep_ref[:, cols] = part[half:]


def values_kernel(sel_ref, w_ref, send_ref, keep_ref):
    quarter = sel_ref.shape[0] // 4
    width = send_ref.shape[1]
    for c in range(0, width, 512):
        cols = slice(c, c + 512)
        part = jnp.dot(
            sel_ref[...], w_ref[:, width + c : width + c + 512], preferred_element_type=jnp.float32
        )
        send_ref[:quarter, cols] = part[:quarter].astype(jnp.bfloat16)
        send_ref[quarter:, cols] = part[2 * quarter : 3 * quarter].astype(jnp.bfloat16)
        keep_ref[:quarter, cols] = part[quarter : 2 * quarter]
        keep_ref[quarter:, cols] = part[3 * quarter :]


def spread_heads(kept_ref, got_ref, cols):
    heads = kept_ref.shape[1] // HDIM
    total = kept_ref[:, cols] + got_ref[:, cols].astype(jnp.float32)
    keys, width = total.shape
    total = total.astype(jnp.bfloat16).astype(jnp.float32)
    head = lax.broadcasted_iota(jnp.int32, (heads, width), 0)
    col = lax.broadcasted_iota(jnp.int32, (heads, width), 1) + cols.start
    mine = (col // HDIM) == head
    blocks = [
        jnp.where(mine, jnp.broadcast_to(total[key : key + 1], (heads, width)), 0.0).astype(
            jnp.bfloat16
        )
        for key in range(keys)
    ]
    return jnp.concatenate(blocks, axis=0)


def probs_kernel(count_ref, q_ref, kept_ref, got_ref, out_ref, wide_ref):
    heads = q_ref.shape[1] // HDIM
    width = q_ref.shape[1]
    for c in range(0, width, 512):
        cols = slice(c, c + 512)
        wide_ref[:, cols] = spread_heads(kept_ref, got_ref, cols)
    count = jnp.broadcast_to(jnp.concatenate([count_ref[:1]] * (out_ref.shape[1] // 128), axis=1), out_ref.shape)
    block = q_ref.shape[0]
    for first in range(0, q_ref.shape[0], block):
        scores = lax.dot_general(
            q_ref[first : first + block],
            wide_ref[...],
            (((1,), (1,)), ((), ())),
            preferred_element_type=jnp.float32,
        )
        scores = scores * SCALE
        key = lax.broadcasted_iota(jnp.int32, scores.shape, 1) // heads
        scores = jnp.where(key < count, scores, NEG)
        parts = [scores[:, c : c + 128] for c in range(0, scores.shape[1], 128)]
        top = functools.reduce(jnp.maximum, parts)
        step = heads
        while step < 128:
            top = jnp.maximum(top, pltpu.roll(top, step, 1))
            step *= 2
        parts = [jnp.exp(p - top) for p in parts]
        total = functools.reduce(jnp.add, parts)
        step = heads
        while step < 128:
            total = total + pltpu.roll(total, step, 1)
            step *= 2
        out_ref[first : first + block] = jnp.concatenate(
            [p / total for p in parts], axis=1
        ).astype(jnp.bfloat16)


def context_kernel(p_ref, kept_ref, got_ref, out_hbm, out_ref, sems):
    chunk = out_ref.shape[1] // sems.shape[0]
    copies = []
    for i in range(sems.shape[0]):
        cols = slice(i * chunk, (i + 1) * chunk)
        out_ref[:, cols] = jnp.dot(
            p_ref[...], spread_heads(kept_ref, got_ref, cols), preferred_element_type=jnp.float32
        ).astype(jnp.bfloat16)
        copies.append(pltpu.make_async_copy(out_ref.at[:, cols], out_hbm.at[:, cols], sems.at[i]))
        copies[-1].start()
    for copy in copies:
        copy.wait()


def select_plan(n, queries, text_rows, null_rows, kv_weight, prompt_lengths, block_owner, uncond_flags):
    features = kv_weight.shape[0]
    width = kv_weight.shape[2]
    rows = queries.shape[0]
    reqs = prompt_lengths.shape[0]
    heads = width // HDIM
    pos = lax.axis_index("seq").astype(jnp.int32)
    smem = pl.BlockSpec(memory_space=pltpu.SMEM)
    vmem = pl.BlockSpec(memory_space=pltpu.VMEM)
    anywhere = pl.BlockSpec(memory_space=pl.ANY)
    params = pltpu.CompilerParams(vmem_limit_bytes=VMEM_LIMIT)
    text_dev = text_rows.shape[0]
    packed = pl.pallas_call(
        functools.partial(pack_kernel, reqs),
        out_shape=jax.ShapeDtypeStruct((n, text_dev, features + 128), jnp.bfloat16),
        in_specs=[smem, smem, anywhere],
        out_specs=anywhere,
        scratch_shapes=[
            pltpu.VMEM((n, text_dev, 128), jnp.bfloat16),
            pltpu.SemaphoreType.DMA((n + 1,)),
        ],
        compiler_params=pltpu.CompilerParams(vmem_limit_bytes=56 * 1024 * 1024),
        name="pack",
    )(block_owner, uncond_flags, text_rows)
    group = [place ^ MIDDLE for place in range(n)]
    held = lax.all_to_all(
        packed, "seq", split_axis=0, concat_axis=0, axis_index_groups=[group], tiled=True
    )
    null_cols = lax.dynamic_slice_in_dim(null_rows, pos * features, features, 1)
    weight = kv_weight.reshape(features, 2 * width)
    half = n * NULL_LEN // 2
    sent = jax.ShapeDtypeStruct((half, width), jnp.bfloat16)
    kept = jax.ShapeDtypeStruct((half, width), jnp.float32)
    estimate = pl.CostEstimate(
        flops=2 * 2 * half * features * width,
        bytes_accessed=2 * features * width,
        transcendentals=0,
    )
    send_k, keep_k, sel, count = pl.pallas_call(
        keys_kernel,
        out_shape=[
            sent,
            kept,
            jax.ShapeDtypeStruct((2 * half, features), jnp.bfloat16),
            jax.ShapeDtypeStruct((8, 128), jnp.int32),
        ],
        in_specs=[smem] + [vmem] * 5,
        out_specs=[vmem] * 4,
        compiler_params=params,
        cost_estimate=estimate,
        name="keys",
    )(
        pos.reshape(1),
        prompt_lengths.reshape(1, reqs),
        null_cols,
        weight,
        held,
        held.reshape(n * text_dev, features + 128),
    )
    send_v, keep_v = pl.pallas_call(
        values_kernel,
        out_shape=[sent, kept],
        in_specs=[vmem] * 2,
        out_specs=[vmem] * 2,
        compiler_params=params,
        cost_estimate=estimate,
        name="values",
    )(sel, weight)

    def reduce_parts(send, keep, masks):
        for mask in masks:
            total = keep + swap(send, n, mask).astype(jnp.float32)
            cut = total.shape[0] // 2
            send, keep = total[:cut].astype(jnp.bfloat16), total[cut:]
        return keep, swap(send, n, 4)

    k_parts = reduce_parts(send_k, keep_k, (2, 1))
    v_parts = reduce_parts(send_v, keep_v, (1, 2))

    lanes = heads * NULL_LEN
    probs = pl.pallas_call(
        probs_kernel,
        out_shape=jax.ShapeDtypeStruct((rows, lanes), jnp.bfloat16),
        in_specs=[vmem] * 4,
        out_specs=vmem,
        scratch_shapes=[pltpu.VMEM((lanes, width), jnp.bfloat16)],
        compiler_params=params,
        cost_estimate=pl.CostEstimate(
            flops=2 * rows * width * lanes, bytes_accessed=2 * rows * width, transcendentals=rows * lanes
        ),
        name="probs",
    )(count, queries, *k_parts)
    return pl.pallas_call(
        context_kernel,
        out_shape=jax.ShapeDtypeStruct((rows, width), jnp.bfloat16),
        in_specs=[vmem] * 3,
        out_specs=anywhere,
        scratch_shapes=[
            pltpu.VMEM((rows, width), jnp.bfloat16),
            pltpu.SemaphoreType.DMA((4,)),
        ],
        compiler_params=params,
        cost_estimate=pl.CostEstimate(
            flops=2 * rows * width * lanes, bytes_accessed=2 * rows * width, transcendentals=0
        ),
        name="context",
    )(probs, *v_parts)


def solution(mesh):
    n = mesh.shape["seq"]

    def per_device(queries, text_rows, null_rows, kv_weight, *rest):
        longest = n * text_rows.shape[0] // 4
        few = n == 8 and longest == NULL_LEN and text_rows.shape[0] == 8
        if few:
            return select_plan(n, queries, text_rows, null_rows, kv_weight, *rest)
        return gather_plan(queries, text_rows, null_rows, kv_weight, *rest)

    placed = (
        P(("groups", "seq"), "head"),
        P(("groups", "seq"), None),
        P(),
        P("seq", None, "head"),
        P("groups"),
        P(("groups", "seq")),
        P(("groups", "seq")),
    )
    return jax.shard_map(
        per_device,
        mesh=mesh,
        in_specs=placed,
        out_specs=P(("groups", "seq"), "head"),
        check_vma=False,
    )
```

```python
import functools

import jax
import jax.numpy as jnp
from jax import lax
from jax.experimental import pallas as pl
from jax.experimental.pallas import tpu as pltpu
from jax.sharding import PartitionSpec as P

HDIM = 128
NULL_LEN = 16
SCALE = HDIM ** (-0.5)
VMEM_LIMIT = 16 * 1024 * 1024
NEG = -1e30


def gather_plan(queries, text_rows, null_rows, kv_weight, prompt_lengths, block_owner, uncond_flags):
    features_dev = kv_weight.shape[0]
    half_width = kv_weight.shape[2]
    text_dev = text_rows.shape[0]
    flat_weight = kv_weight.reshape(features_dev, 2 * half_width)
    text_cols = lax.all_to_all(text_rows, "seq", split_axis=1, concat_axis=0, tiled=True)
    own_rows = lax.psum_scatter(
        jnp.dot(text_cols, flat_weight, preferred_element_type=jnp.float32),
        "seq",
        scatter_dimension=0,
        tiled=True,
    )
    null_cols = lax.dynamic_slice_in_dim(
        null_rows, lax.axis_index("seq") * features_dev, features_dev, 1
    )
    null_part = jnp.dot(null_cols, flat_weight, preferred_element_type=jnp.float32)
    null_sum = lax.psum(null_part, "seq")
    own_kv = own_rows.astype(jnp.bfloat16).reshape(text_dev, 2, half_width)
    null_kv = null_sum.astype(jnp.bfloat16).reshape(NULL_LEN, 2, half_width)
    all_text = lax.all_gather(own_kv, "seq", axis=0, tiled=True)
    text_total = all_text.shape[0]
    heads_dev = half_width // HDIM
    keys_local = jnp.concatenate([all_text[:, 0], null_kv[:, 0]], axis=0).reshape(
        -1, heads_dev, HDIM
    )
    values_local = jnp.concatenate([all_text[:, 1], null_kv[:, 1]], axis=0).reshape(
        -1, heads_dev, HDIM
    )
    prompt_ends = jnp.cumsum(prompt_lengths)
    text_index = jnp.arange(text_total, dtype=jnp.int32)
    segment = jnp.sum((text_index[:, None] >= prompt_ends[None, :]).astype(jnp.int32), axis=1)
    segment_all = jnp.concatenate([segment, jnp.full((NULL_LEN,), -1, jnp.int32)])
    is_null = jnp.arange(text_total + NULL_LEN, dtype=jnp.int32) >= text_total
    allowed = jnp.where(uncond_flags[0] == 1, is_null, segment_all == block_owner[0])
    row_count = queries.shape[0]
    query_heads = queries.reshape(row_count, heads_dev, HDIM)
    scores = (
        jnp.einsum("qhd,khd->hqk", query_heads, keys_local, preferred_element_type=jnp.float32)
        * SCALE
    )
    scores = jnp.where(allowed[None, None, :], scores, jnp.float32(NEG))
    row_max = jnp.max(scores, axis=-1, keepdims=True)
    weights_exp = jnp.exp(scores - row_max)
    row_total = jnp.sum(weights_exp, axis=-1, keepdims=True)
    probs = (weights_exp / row_total).astype(jnp.bfloat16)
    context = jnp.einsum("hqk,khd->qhd", probs, values_local, preferred_element_type=jnp.float32)
    return context.reshape(row_count, half_width).astype(jnp.bfloat16)


def swap(x, n, mask):
    return lax.ppermute(x, "seq", [(i, i ^ mask) for i in range(n)])


TARGETS = (7, 3, 5, 1, 6, 2, 4, 0)
MIDDLE = 4


def keys_kernel(
    pos_ref, len_ref, null_ref, w_ref, code_ref, rows_ref, send_ref, keep_ref, sel_ref, count_ref
):
    features = null_ref.shape[1]
    rows = sel_ref.shape[0]
    total = rows_ref.shape[0]
    text_dev = code_ref.shape[1]
    text = rows_ref[:, :features]
    text = jnp.concatenate([text, jnp.zeros((rows - total, features), text.dtype)], axis=0)
    codes = []
    for m in TARGETS:
        code = code_ref[jnp.bitwise_xor(pos_ref[0], m ^ MIDDLE)][:, features:].astype(jnp.float32)
        codes += [code] * (NULL_LEN // text_dev)
    code = jnp.concatenate(codes, axis=0)
    reqs = len_ref.shape[1]
    uncond = code >= reqs
    owner = jnp.where(uncond, code - reqs, code)[:, :reqs]
    request = lax.broadcasted_iota(jnp.int32, owner.shape, 1).astype(jnp.float32)
    lengths = jnp.broadcast_to(len_ref[...].astype(jnp.float32), owner.shape)
    start = jnp.sum(jnp.where(request < owner, lengths, 0.0), axis=1, keepdims=True)
    length = jnp.sum(jnp.where(request == owner, lengths, 0.0), axis=1, keepdims=True)
    length = jnp.where(uncond, NULL_LEN, jnp.broadcast_to(length, uncond.shape))
    own = rows - NULL_LEN
    count_ref[...] = length[own : own + 8].astype(jnp.int32)
    row = lax.broadcasted_iota(jnp.int32, code.shape, 0) % NULL_LEN
    col = jnp.bitwise_xor(lax.broadcasted_iota(jnp.int32, code.shape, 1), MIDDLE * text_dev)
    pick = col.astype(jnp.float32) == start + row.astype(jnp.float32)
    pick = pick.astype(jnp.float32).astype(jnp.bfloat16)
    text_sel = jnp.dot(pick, text, preferred_element_type=jnp.float32)
    null_sel = jnp.concatenate([null_ref[...].astype(jnp.float32)] * (rows // NULL_LEN), axis=0)
    wide = jnp.concatenate([uncond] * (features // 128), axis=1)
    sel = jnp.where(wide, null_sel, text_sel).astype(jnp.bfloat16)
    sel_ref[...] = sel
    half = rows // 2
    width = send_ref.shape[1]
    for c in range(0, width, 512):
        cols = slice(c, c + 512)
        part = jnp.dot(sel, w_ref[:, cols], preferred_element_type=jnp.float32)
        send_ref[:, cols] = part[:half].astype(jnp.bfloat16)
        keep_ref[:, cols] = part[half:]


def values_kernel(sel_ref, w_ref, send_ref, keep_ref):
    quarter = sel_ref.shape[0] // 4
    width = send_ref.shape[1]
    for c in range(0, width, 512):
        cols = slice(c, c + 512)
        part = jnp.dot(
            sel_ref[...], w_ref[:, width + c : width + c + 512], preferred_element_type=jnp.float32
        )
        send_ref[:quarter, cols] = part[:quarter].astype(jnp.bfloat16)
        send_ref[quarter:, cols] = part[2 * quarter : 3 * quarter].astype(jnp.bfloat16)
        keep_ref[:quarter, cols] = part[quarter : 2 * quarter]
        keep_ref[quarter:, cols] = part[3 * quarter :]


def spread_heads(kept_ref, got_ref, cols):
    heads = kept_ref.shape[1] // HDIM
    total = kept_ref[:, cols] + got_ref[:, cols].astype(jnp.float32)
    keys, width = total.shape
    total = total.astype(jnp.bfloat16).astype(jnp.float32)
    head = lax.broadcasted_iota(jnp.int32, (heads, width), 0)
    col = lax.broadcasted_iota(jnp.int32, (heads, width), 1) + cols.start
    mine = (col // HDIM) == head
    blocks = [
        jnp.where(mine, jnp.broadcast_to(total[key : key + 1], (heads, width)), 0.0).astype(
            jnp.bfloat16
        )
        for key in range(keys)
    ]
    return jnp.concatenate(blocks, axis=0)


def probs_kernel(count_ref, q_ref, kept_ref, got_ref, out_ref, wide_ref, scores_ref):
    heads = q_ref.shape[1] // HDIM
    width = q_ref.shape[1]
    for c in range(0, width, 512):
        cols = slice(c, c + 512)
        wide_ref[:, cols] = spread_heads(kept_ref, got_ref, cols)
    scores_ref[...] = lax.dot_general(
        q_ref[...], wide_ref[...], (((1,), (1,)), ((), ())), preferred_element_type=jnp.float32
    )
    block = 128
    lanes = out_ref.shape[1]
    count = jnp.concatenate([count_ref[:1]] * (lanes // 128), axis=1)
    count = jnp.broadcast_to(count, (block, lanes))
    for first in range(0, q_ref.shape[0], block):
        scores = scores_ref[first : first + block]
        scores = scores * SCALE
        key = lax.broadcasted_iota(jnp.int32, scores.shape, 1) // heads
        scores = jnp.where(key < count, scores, NEG)
        parts = [scores[:, c : c + 128] for c in range(0, scores.shape[1], 128)]
        top = functools.reduce(jnp.maximum, parts)
        step = heads
        while step < 128:
            top = jnp.maximum(top, pltpu.roll(top, step, 1))
            step *= 2
        parts = [jnp.exp(p - top) for p in parts]
        total = functools.reduce(jnp.add, parts)
        step = heads
        while step < 128:
            total = total + pltpu.roll(total, step, 1)
            step *= 2
        out_ref[first : first + block] = jnp.concatenate(
            [p / total for p in parts], axis=1
        ).astype(jnp.bfloat16)


def context_kernel(p_ref, kept_ref, got_ref, out_hbm, out_ref, sems):
    chunk = out_ref.shape[1] // sems.shape[0]
    copies = []
    for i in range(sems.shape[0]):
        cols = slice(i * chunk, (i + 1) * chunk)
        out_ref[:, cols] = jnp.dot(
            p_ref[...], spread_heads(kept_ref, got_ref, cols), preferred_element_type=jnp.float32
        ).astype(jnp.bfloat16)
        copies.append(pltpu.make_async_copy(out_ref.at[:, cols], out_hbm.at[:, cols], sems.at[i]))
        copies[-1].start()
    for copy in copies:
        copy.wait()


def select_plan(n, queries, text_rows, null_rows, kv_weight, prompt_lengths, block_owner, uncond_flags):
    features = kv_weight.shape[0]
    width = kv_weight.shape[2]
    rows = queries.shape[0]
    reqs = prompt_lengths.shape[0]
    heads = width // HDIM
    pos = lax.axis_index("seq").astype(jnp.int32)
    smem = pl.BlockSpec(memory_space=pltpu.SMEM)
    vmem = pl.BlockSpec(memory_space=pltpu.VMEM)
    anywhere = pl.BlockSpec(memory_space=pl.ANY)
    params = pltpu.CompilerParams(vmem_limit_bytes=VMEM_LIMIT)
    text_dev = text_rows.shape[0]
    code = (block_owner[0] + reqs * uncond_flags[0]).astype(jnp.bfloat16)
    text = text_rows.reshape(text_dev, n, features).transpose(1, 0, 2)
    text = jnp.concatenate([text[MIDDLE:], text[:MIDDLE]], axis=0)
    packed = jnp.concatenate([text, jnp.full((n, text_dev, 128), code, jnp.bfloat16)], axis=2)
    group = [place ^ MIDDLE for place in range(n)]
    held = lax.all_to_all(
        packed, "seq", split_axis=0, concat_axis=0, axis_index_groups=[group], tiled=True
    )
    null_cols = lax.dynamic_slice_in_dim(null_rows, pos * features, features, 1)
    weight = kv_weight.reshape(features, 2 * width)
    half = n * NULL_LEN // 2
    sent = jax.ShapeDtypeStruct((half, width), jnp.bfloat16)
    kept = jax.ShapeDtypeStruct((half, width), jnp.float32)
    estimate = pl.CostEstimate(
        flops=2 * 2 * half * features * width,
        bytes_accessed=2 * features * width,
        transcendentals=0,
    )
    send_k, keep_k, sel, count = pl.pallas_call(
        keys_kernel,
        out_shape=[
            sent,
            kept,
            jax.ShapeDtypeStruct((2 * half, features), jnp.bfloat16),
            jax.ShapeDtypeStruct((8, 128), jnp.int32),
        ],
        in_specs=[smem] + [vmem] * 5,
        out_specs=[vmem] * 4,
        compiler_params=params,
        cost_estimate=estimate,
        name="keys",
    )(
        pos.reshape(1),
        prompt_lengths.reshape(1, reqs),
        null_cols,
        weight,
        held,
        held.reshape(n * text_dev, features + 128),
    )
    send_v, keep_v = pl.pallas_call(
        values_kernel,
        out_shape=[sent, kept],
        in_specs=[vmem] * 2,
        out_specs=[vmem] * 2,
        compiler_params=params,
        cost_estimate=estimate,
        name="values",
    )(sel, weight)

    def reduce_parts(send, keep, masks):
        for mask in masks:
            total = keep + swap(send, n, mask).astype(jnp.float32)
            cut = total.shape[0] // 2
            send, keep = total[:cut].astype(jnp.bfloat16), total[cut:]
        return keep, swap(send, n, 4)

    k_parts = reduce_parts(send_k, keep_k, (1, 2))
    v_parts = reduce_parts(send_v, keep_v, (2, 1))

    lanes = heads * NULL_LEN
    probs = pl.pallas_call(
        probs_kernel,
        out_shape=jax.ShapeDtypeStruct((rows, lanes), jnp.bfloat16),
        in_specs=[vmem] * 4,
        out_specs=vmem,
        scratch_shapes=[
            pltpu.VMEM((lanes, width), jnp.bfloat16),
            pltpu.VMEM((rows, lanes), jnp.float32),
        ],
        compiler_params=params,
        cost_estimate=pl.CostEstimate(
            flops=2 * rows * width * lanes, bytes_accessed=2 * rows * width, transcendentals=rows * lanes
        ),
        name="probs",
    )(count, queries, *k_parts)
    return pl.pallas_call(
        context_kernel,
        out_shape=jax.ShapeDtypeStruct((rows, width), jnp.bfloat16),
        in_specs=[vmem] * 3,
        out_specs=anywhere,
        scratch_shapes=[
            pltpu.VMEM((rows, width), jnp.bfloat16),
            pltpu.SemaphoreType.DMA((4,)),
        ],
        compiler_params=params,
        cost_estimate=pl.CostEstimate(
            flops=2 * rows * width * lanes, bytes_accessed=2 * rows * width, transcendentals=0
        ),
        name="context",
    )(probs, *v_parts)


def solution(mesh):
    n = mesh.shape["seq"]

    def per_device(queries, text_rows, null_rows, kv_weight, *rest):
        longest = n * text_rows.shape[0] // 4
        few = n == 8 and longest == NULL_LEN and text_rows.shape[0] == 8
        if few:
            return select_plan(n, queries, text_rows, null_rows, kv_weight, *rest)
        return gather_plan(queries, text_rows, null_rows, kv_weight, *rest)

    placed = (
        P(("groups", "seq"), "head"),
        P(("groups", "seq"), None),
        P(),
        P("seq", None, "head"),
        P("groups"),
        P(("groups", "seq")),
        P(("groups", "seq")),
    )
    return jax.shard_map(
        per_device,
        mesh=mesh,
        in_specs=placed,
        out_specs=P(("groups", "seq"), "head"),
        check_vma=False,
    )
```
